512 devices in a mesh: section: 4 (over x), bins: 128 (over y, z, core).
Axes of the slice: x: 4, y: 4, z: 16, core: 2. Of those that a mesh axis runs over, the one named last changes fastest.
Arguments:
- traces: float32 [8192, 4096], P('bins', 'section'), may hold values from -6 to 6
- filters: float32 [128, 256], P('bins'), may hold values from -0.375 to 0.375
- owners: int32 [8192, 1], P('bins'), may hold values from 0 to 127; in each aligned block of 64 rows (0 to 63, 64 to 127, ...) at most 2 rows name the same one
- sub_bins: int32 [8192], P('bins'), may hold values from 0 to 7
- sample_map: int32 [8192, 4096], P('bins', 'section'), may hold values from 0 to 1019
Outputs:
- stack: float32 [1024, 4096], P('bins', 'section')
The draws below stay inside these ranges and needn't reach their ends.
Inputs may be any that keep to these rules, and one draw needn't show every extreme that they name: `owners`: in each aligned block of 64 rows (the traces of one shot) no owner is named more than 2 times; in some block one owner is named exactly 2 times.
All inputs are finite; a program needn't handle non-finite values.
Results may differ from the reference program's by a relative error of at most 0.0003.
Values sent between devices are 32-bit elements; how exact they have to be, the bound alone decides.
No kernel may reach another device: no remote copies, remote signals or barrier semaphores. Data moves between devices by JAX's collectives and lax.ppermute only.
A program may use at most 64 MiB of HBM per device.

```python
import math
import jax
import jax.numpy as jnp
import numpy as np
from jax import lax

NS = 4096
TAPS = 256
BAND = 256
TR_DEV = 64
BIN_DEV = 8
SHOTS = 128
NTR = 8192
CAP = 2
N_BINS = 128


def draw_sample_map(key, part):
    key = jax.random.fold_in(key, 7)
    shifts = jax.random.randint(key, (NTR, NS), 0, 4 * (BAND - 1), dtype=jnp.int32)
    shifts = shifts.at[0, 0].set(0).at[0, NS - 1].set(4 * (BAND - 1) - 1)
    return shifts


def place_ends(values, rng, low, top_value):
    longest = values.shape.index(max(values.shape))
    spots = []
    for shift in (0, 1):
        where = [jax.random.randint(jax.random.fold_in(rng, axis), (), 0, length) for axis, length in enumerate(values.shape)]
        where[longest] = (where[longest] + shift) % values.shape[longest]
        spots.append(tuple(where))
    return values.at[spots[0]].set(low).at[spots[1]].set(top_value)


def levels(rng, extent, split, least, high):
    gain = 1.0
    for axis_at, shards_of in split:
        steps = jax.random.uniform(jax.random.fold_in(jax.random.fold_in(rng, 6), axis_at), (shards_of,), jnp.float32, least / len(split), high / len(split))
        gain = gain * jnp.repeat(jnp.exp(steps), extent[axis_at] // shards_of).reshape((-1,) + (1,) * (len(extent) - 1 - axis_at))
    return gain


def deal_out(key, own, number, rows, number_of, top, most, slope):
    order = jax.random.permutation(key, number_of)
    packed, common = portions_of(number_of, rows * top, most, slope, True), portions_of(number_of, rows * top, most, slope, False)
    places = jnp.arange(number_of)

    def named(lengths, turn):
        used = int((lengths > 0).sum())
        fixed = max(1, used // 4)
        moved = fixed + (places - fixed + turn * (used - fixed)) % max(1, number_of - fixed)
        return jnp.zeros((number_of,), jnp.int32).at[order[jnp.where(places < fixed, places, moved)]].set(jnp.asarray(lengths, jnp.int32))

    lengths = jnp.where(number % 4 == 0, named(packed, number // 4), named(common, number - number // 4 - 1))
    mixed = jax.random.permutation(jax.random.fold_in(own, 3), number_of)
    giver, receiver = mixed[0:number_of // 2 * 2:2], mixed[1:number_of // 2 * 2:2]
    room = jnp.minimum(lengths[giver] - 1, most - lengths[receiver]) // 2
    room = jnp.where((giver == order[0]) | (receiver == order[0]) | (lengths[receiver] == 0), 0, jnp.maximum(room, 0))
    moved = jax.random.randint(jax.random.fold_in(own, 4), (number_of // 2,), 0, 1 << 20) % (room + 1)
    lengths = lengths.at[giver].add(-moved).at[receiver].add(moved)
    members = jnp.searchsorted(jnp.cumsum(lengths), jnp.arange(rows * top), side="right").astype(jnp.int32)
    listing = members.reshape(top, rows).T
    listing = listing[jax.random.permutation(jax.random.fold_in(own, 1), rows)]
    turn = jax.random.randint(jax.random.fold_in(own, 2), (rows, 1), 0, top)
    return jnp.take_along_axis(listing, (jnp.arange(top)[None, :] + turn) % top, axis=1)


def portions_of(count, total, reach, slope, full):
    loads = [(1 << 20) // math.isqrt(standing ** slope) + 1 for standing in range(1, count + 1)]
    largest = reach if full else min(reach, max(-(-total // count), total * loads[0] // sum(loads)))
    least = 1 if total - largest >= count - 1 else 0
    given, rest = [largest] + [least] * (count - 1), total - largest - least * (count - 1)
    while rest > 0:
        movable = [i for i in range(1, count) if given[i] < largest] or [i for i in range(1, count) if given[i] < reach]
        mass, budget = sum([loads[i] for i in movable]), rest
        for i in movable:
            addition = min(reach - given[i], max(1, budget * loads[i] // mass), rest)
            given[i] = given[i] + addition
            rest = rest - addition
    return np.array(given)


def gaussian(rng, extent, spread, limit, shards=(), kind=jnp.bfloat16):
    loudness = levels(rng, extent, shards, -0.22, 0.18) if shards else 1.0
    array = jax.random.normal(rng, extent, jnp.float32) * spread * loudness
    return jnp.minimum(jnp.maximum(array, -limit), limit).astype(kind)


def setup_inputs(seed: int = 0) -> dict:
    keys = jax.random.split(jax.random.key(seed), 6)
    traces = gaussian(keys[0], (NTR, NS), 1.0, 6.0, ((0, 128), (1, 4)), jnp.float32)
    filters = gaussian(keys[1], (SHOTS, TAPS), TAPS ** -0.5, 0.375, ((0, 128),), jnp.float32)
    owners_keys = jax.random.split(jax.random.fold_in(keys[2], 1), NTR // TR_DEV)
    owners_turns = jax.random.permutation(jax.random.fold_in(keys[2], 3), NTR // TR_DEV)
    owners = jax.vmap(lambda own, number: deal_out(jax.random.fold_in(keys[2], 2), own, number, TR_DEV, N_BINS, 1, CAP, 2))(owners_keys, owners_turns).reshape((NTR, 1))
    sub_bins = place_ends(jax.random.randint(keys[3], (NTR,), 0, BIN_DEV), jax.random.fold_in(keys[3], 1), 0, BIN_DEV - 1).astype(jnp.int32)
    sample_map = draw_sample_map(jax.random.fold_in(keys[5], 71), 0)
    return {"traces": traces, "filters": filters, "owners": owners, "sub_bins": sub_bins, "sample_map": sample_map}


def toeplitz_pair(filt):
    taps = filt.shape[0]
    zeros = jnp.zeros((taps,), filt.dtype)
    padded = jnp.concatenate([zeros, filt, zeros])
    starts = jnp.arange(taps, dtype=jnp.int32)

    def lower_row(j):
        return lax.dynamic_slice_in_dim(padded, (taps - j).astype(jnp.int32), taps)

    def upper_row(j):
        return lax.dynamic_slice_in_dim(padded, (2 * taps - j).astype(jnp.int32), taps)
    return (jax.vmap(lower_row)(starts), jax.vmap(upper_row)(starts))

def deconvolve(current, previous, lower, upper):
    first = jnp.einsum('rbj,ji->rbi', current, lower, precision=lax.Precision.HIGHEST)
    second = jnp.einsum('rbj,ji->rbi', previous, upper, precision=lax.Precision.HIGHEST)
    return first + second

def move_out(window, quarter, anchor):
    whole = (quarter // 4 - anchor).astype(jnp.int32)
    weight = (quarter % 4).astype(jnp.float32) * 0.25
    near = jnp.take_along_axis(window, whole, axis=1)
    far = jnp.take_along_axis(window, whole + 1, axis=1)
    return near + weight * (far - near)

def reference(traces, filters, owners, sub_bins, sample_map):
    shots = filters.shape[0]
    taps = filters.shape[1]
    rows = traces.shape[0] // shots
    width = traces.shape[1]
    total_bins = BIN_DEV * shots
    times = 4 * jnp.arange(width, dtype=jnp.int32)

    def one_shot(carry, index):
        sums, counts = carry
        start = (index * rows).astype(jnp.int32)
        raw = lax.dynamic_slice_in_dim(traces, start, rows, 0)
        quarter = lax.dynamic_slice_in_dim(sample_map, start, rows, 0) + times[None, :]
        owner = lax.dynamic_slice_in_dim(owners[:, 0], start, rows, 0)
        sub = lax.dynamic_slice_in_dim(sub_bins, start, rows, 0)
        lower, upper = toeplitz_pair(filters[index])
        blocks = raw.reshape(rows, width // taps, taps)
        previous = jnp.concatenate([jnp.zeros((rows, 1, taps), raw.dtype), blocks[:, :-1]], axis=1)
        deconvolved = deconvolve(blocks, previous, lower, upper).reshape(rows, width)
        window = jnp.concatenate([deconvolved, jnp.zeros((rows, taps), raw.dtype)], axis=1)
        corrected = move_out(window, quarter, 0)
        label = owner * BIN_DEV + sub
        sums = sums + jax.ops.segment_sum(corrected, label, num_segments=total_bins)
        counts = counts + jax.ops.segment_sum(jnp.ones((rows,), jnp.int32), label, num_segments=total_bins)
        return ((sums, counts), None)
    init = (jnp.zeros((total_bins, width), traces.dtype), jnp.zeros((total_bins,), jnp.int32))
    (sums, counts), _ = lax.scan(one_shot, init, jnp.arange(shots, dtype=jnp.int32))
    scale = jnp.sqrt(jnp.maximum(counts, 1).astype(traces.dtype))
    return sums / scale[:, None]
```

```python
import functools

import jax
import jax.numpy as jnp
import numpy as np
from jax import lax
from jax.experimental import pallas as pl
from jax.experimental.pallas import tpu as pltpu
from jax.sharding import Mesh
from jax.sharding import PartitionSpec as P

BIN_DEV = 8
LANES = 128
NY, NZ, NC = 4, 16, 2
BINS = ("y", "z", "c")


def halves(value):
    high = value.astype(jnp.bfloat16)
    low = (value - high.astype(jnp.float32)).astype(jnp.bfloat16)
    return high, low


def dot(a, b):
    return jnp.dot(a, b, preferred_element_type=jnp.float32)


def correct_kernel(last_ref, traces_ref, before_ref, after_ref, filter_ref, label_ref, map_ref, out_ref):
    rows, width = traces_ref.shape
    taps = filter_ref.shape[1]
    count = width // taps
    padded = jnp.concatenate([filter_ref[...], jnp.zeros((1, taps), jnp.float32)], axis=1)
    shifted = pltpu.roll(jnp.broadcast_to(padded, (taps, 2 * taps)), 0, 1, stride=1, stride_axis=0)
    toeplitz_high, toeplitz_low = halves(shifted)
    blocks = [before_ref[...]]
    blocks += [traces_ref[:, b * taps : (b + 1) * taps] for b in range(count)]
    blocks += [after_ref[...]]
    stacked_high, stacked_low = halves(jnp.concatenate(blocks, axis=0))
    spread = dot(stacked_high, toeplitz_high) + (dot(stacked_low, toeplitz_high) + dot(stacked_high, toeplitz_low))
    pieces = []
    for b in range(1, count + 2):
        piece = spread[b * rows : (b + 1) * rows, :taps] + spread[(b - 1) * rows : b * rows, taps:]
        if b == count + 1:
            piece = jnp.where(last_ref[0] == 1, 0.0, piece)
        pieces.append(piece)
    window = jnp.concatenate(pieces, axis=1)
    span = window.shape[1]
    step = pltpu.roll(window, span - 1, 1) - window
    lane = lax.broadcasted_iota(jnp.int32, (rows, LANES), 1)
    for c in range(width // LANES):
        quarter = map_ref[:, c * LANES : (c + 1) * LANES]
        place = lane + (quarter >> 2)
        weight = (quarter & 3).astype(jnp.float32) * 0.25
        inside = place & (LANES - 1)
        block = place >> 7
        near = far = None
        for k in range(3):
            columns = slice((c + k) * LANES, (c + k + 1) * LANES)
            value = jnp.take_along_axis(window[:, columns], inside, axis=1, mode="promise_in_bounds")
            slope = jnp.take_along_axis(step[:, columns], inside, axis=1, mode="promise_in_bounds")
            near = value if k == 0 else jnp.where(block == k, value, near)
            far = slope if k == 0 else jnp.where(block == k, slope, far)
        moved = near + weight * far
        for y in range(NY):
            out_ref[y, c * rows : (c + 1) * rows, :] = moved
    for y in range(NY):
        out_ref[y, width // LANES * rows :, :] = label_ref[...]


def combine_kernel(first_ref, arrived_ref, *refs):
    out_ref = refs[-1]
    parts = out_ref.shape[1] // BIN_DEV - 1
    rows = (arrived_ref.shape[1] - BIN_DEV) // parts
    tile = arrived_ref[0, parts * rows :, :]
    for y in range(1, NY):
        tile = tile + arrived_ref[y, parts * rows :, :]
    labels = jnp.concatenate([tile[0:1, :], tile[1:2, :]], axis=1)
    row = lax.broadcasted_iota(jnp.int32, (NZ * BIN_DEV, 1), 0)
    number = first_ref[0] + (row // BIN_DEV) * (NC * BIN_DEV) + row % BIN_DEV
    hit = labels == number.astype(jnp.float32)
    member = jnp.where(hit, 1.0, 0.0).astype(jnp.bfloat16)
    for c in range(parts):
        piece = jnp.concatenate([arrived_ref[y, c * rows : (c + 1) * rows, :] for y in range(NY)], axis=0)
        high, low = halves(piece)
        total = (dot(member, high) + dot(member, low)).reshape(NZ, BIN_DEV, LANES)
        if len(refs) == 2:
            total = total + refs[0][:, c * BIN_DEV : (c + 1) * BIN_DEV, :]
        out_ref[:, c * BIN_DEV : (c + 1) * BIN_DEV, :] = total
    fold = dot(member, jnp.ones((NY * rows, LANES), jnp.bfloat16)).reshape(NZ, BIN_DEV, LANES)
    if len(refs) == 2:
        fold = fold + refs[0][:, parts * BIN_DEV :, :]
    out_ref[:, parts * BIN_DEV :, :] = fold


def finish_kernel(arrived_ref, out_ref):
    total = arrived_ref[0]
    for z in range(1, NZ):
        total = total + arrived_ref[z]
    parts = total.shape[0] // BIN_DEV - 1
    scale = jnp.sqrt(jnp.maximum(total[parts * BIN_DEV :, :], 1.0))
    for c in range(parts):
        out_ref[:, c * LANES : (c + 1) * LANES] = total[c * BIN_DEV : (c + 1) * BIN_DEV, :] / scale


VMEM = pl.BlockSpec(memory_space=pltpu.VMEM)
SMEM = pl.BlockSpec(memory_space=pltpu.SMEM)


def call(kernel, shape, name, *operands):
    specs = [SMEM if operand.dtype == jnp.int32 and operand.ndim == 1 else VMEM for operand in operands]
    return pl.pallas_call(
        kernel,
        out_shape=jax.ShapeDtypeStruct(shape, jnp.float32),
        in_specs=specs,
        out_specs=VMEM,
        name=name,
        compiler_params=pltpu.CompilerParams(vmem_limit_bytes=40 * 1024 * 1024),
    )(*operands)


def passed_along(value, axis, steps):
    count = lax.axis_size(axis)
    leading, last = (max(0, -steps), min(count, count - steps))
    return lax.ppermute(value, axis, [(source, source + steps) for source in range(leading, last)])


def per_device(traces, filters, owners, sub_bins, sample_map):
    rows, width = traces.shape
    taps = filters.shape[1]
    parts = width // LANES
    before = passed_along(traces[:, width - taps :], "section", 1)
    after = passed_along(traces[:, :taps], "section", -1)
    y, c = lax.axis_index("y"), lax.axis_index("c")
    last = (lax.axis_index("section") == lax.axis_size("section") - 1).astype(jnp.int32).reshape(1)
    label = (owners[:, 0] * BIN_DEV + sub_bins).astype(jnp.float32)
    tile = lax.dynamic_update_slice(jnp.zeros((BIN_DEV, LANES), jnp.float32), label[None, :], (y // 2, (y % 2) * rows))
    sent = call(
        correct_kernel, (NY, parts * rows + BIN_DEV, LANES), "correct",
        last, traces, before, after, filters, tile, sample_map,
    )
    gathered = lax.all_to_all(sent, "y", split_axis=0, concat_axis=0, tiled=True)
    shape = (NZ, (parts + 1) * BIN_DEV, LANES)

    def first(core):
        return ((y * NZ * NC + core) * BIN_DEV).astype(jnp.int32).reshape(1)

    other = call(combine_kernel, shape, "combine_other", first(1 - c), gathered)
    other = lax.ppermute(other, "c", [(0, 1), (1, 0)])
    summed = call(combine_kernel, shape, "combine_own", first(c), gathered, other)
    arrived = lax.all_to_all(summed, "z", split_axis=0, concat_axis=0, tiled=True)
    return call(finish_kernel, (BIN_DEV, width), "finish", arrived)


def solution(mesh):
    fine = Mesh(mesh.devices.reshape(mesh.devices.shape[0], NY, NZ, NC), ("section",) + BINS)
    in_specs = (
        P(BINS, "section"),
        P(BINS, None),
        P(BINS, None),
        P(BINS),
        P(BINS, "section"),
    )
    return jax.shard_map(
        per_device, mesh=fine, in_specs=in_specs, out_specs=P(BINS, "section"), check_vma=False
    )
```

```python
import functools

import jax
import jax.numpy as jnp
from jax import lax
from jax.experimental import pallas as pl
from jax.experimental.pallas import tpu as pltpu
from jax.sharding import Mesh
from jax.sharding import PartitionSpec as P

BIN_DEV = 8
CAP = 2
LANES = 128
NY, NU, NW, NC = 4, 8, 2, 2
BINS = ("y", "u", "w", "c")
NEAR = ("y", "w", "c")
PEERS = NY * NW * NC
SLOTS = NU * CAP


def halves(value):
    high = value.astype(jnp.bfloat16)
    low = (value - high.astype(jnp.float32)).astype(jnp.bfloat16)
    return high, low


def dot(a, b):
    return jnp.dot(a, b, preferred_element_type=jnp.float32)


def dot_split(a, b):
    return dot(a[0], b[0]) + (dot(a[1], b[0]) + dot(a[0], b[1]))


def move_out(window, quarters):
    rows, span = window.shape
    step = pltpu.roll(window, span - 1, 1) - window
    lane = lax.broadcasted_iota(jnp.int32, (rows, LANES), 1)
    moved = []
    for c, quarter in enumerate(quarters):
        place = lane + (quarter >> 2)
        weight = (quarter & 3).astype(jnp.float32) * 0.25
        inside = place & (LANES - 1)
        block = place >> 7
        near = slope = None
        for k in range(3):
            columns = slice((c + k) * LANES, (c + k + 1) * LANES)
            value = jnp.take_along_axis(window[:, columns], inside, axis=1, mode="promise_in_bounds")
            change = jnp.take_along_axis(step[:, columns], inside, axis=1, mode="promise_in_bounds")
            near = value if k == 0 else jnp.where(block == k, value, near)
            slope = change if k == 0 else jnp.where(block == k, change, slope)
        moved.append(near + weight * slope)
    return jnp.concatenate(moved, axis=1)


def place_slots(slot, moved, target_ref, start):
    rows = moved.shape[0]
    number = lax.broadcasted_iota(jnp.int32, (PEERS * SLOTS, rows), 0)
    member = jnp.where(number == slot, 1.0, 0.0).astype(jnp.bfloat16)
    high, low = halves(moved)
    placed = dot(member, high) + dot(member, low)
    for c in range(moved.shape[1] // LANES):
        piece = placed[:, c * LANES : (c + 1) * LANES].reshape(PEERS, SLOTS, LANES)
        target_ref[:, start + c * SLOTS : start + (c + 1) * SLOTS, :] = piece


def inner_kernel(
    place_ref, traces_hbm, map_hbm, filter_hbm, owner_hbm, sub_hbm,
    out_hbm, high_ref, low_ref, edge_ref, edge_map_ref, slot_ref,
    traces_ref, map_ref, filter_ref, owner_ref, sub_ref, stage_ref, sems, out_sems,
):
    rows, width = traces_ref.shape
    taps = filter_ref.shape[1]
    half = width // 2
    loads = [
        pltpu.make_async_copy(filter_hbm, filter_ref, sems.at[0]),
        pltpu.make_async_copy(owner_hbm, owner_ref, sems.at[1]),
        pltpu.make_async_copy(sub_hbm, sub_ref, sems.at[2]),
        pltpu.make_async_copy(traces_hbm, traces_ref, sems.at[3]),
        pltpu.make_async_copy(map_hbm.at[:, taps : taps + half], map_ref, sems.at[4]),
        pltpu.make_async_copy(map_hbm.at[:, :taps], edge_map_ref.at[:, :taps], sems.at[5]),
        pltpu.make_async_copy(map_hbm.at[:, taps + half :], edge_map_ref.at[:, taps:], sems.at[6]),
    ]
    for load in loads:
        load.start()
    loads[0].wait()
    padded = jnp.concatenate([filter_ref[...], jnp.zeros((1, taps), jnp.float32)], axis=1)
    shifted = pltpu.roll(jnp.broadcast_to(padded, (taps, 2 * taps)), 0, 1, stride=1, stride_axis=0)
    toeplitz = halves(shifted)
    high_ref[...], low_ref[...] = toeplitz

    loads[1].wait()
    loads[2].wait()
    owner, sub = owner_ref[...], sub_ref[...]
    owners = NY * NU * NW * NC
    named = lax.broadcasted_iota(jnp.int32, (owners, rows), 0) == owner
    named = jnp.where(named, 1.0, 0.0)
    earlier = lax.broadcasted_iota(jnp.int32, (rows, rows), 0) < lax.broadcasted_iota(jnp.int32, (rows, rows), 1)
    earlier = jnp.where(earlier, 1.0, 0.0).astype(jnp.bfloat16)
    rank = jnp.sum(named * dot(named.astype(jnp.bfloat16), earlier), axis=0, keepdims=True).astype(jnp.int32)
    core, w = owner % NC, owner // NC % NW
    u, y = owner // (NC * NW) % NU, owner // (NC * NW * NU)
    peer = (y * NW + w) * NC + core
    within = u * CAP + rank
    slot = peer * SLOTS + within
    slot_ref[...] = slot
    to_peer = lax.broadcasted_iota(jnp.int32, (PEERS, rows), 0) == peer
    to_peer = jnp.where(to_peer, (sub + 1).astype(jnp.float32), 0.0).astype(jnp.bfloat16)
    column = lax.broadcasted_iota(jnp.int32, (PEERS * SLOTS, rows), 0)
    in_column = jnp.where(column == within + place_ref[0] * SLOTS, 1.0, 0.0).astype(jnp.bfloat16)
    labels = lax.dot_general(to_peer, in_column, (((1,), (1,)), ((), ())), preferred_element_type=jnp.float32)
    first = lax.broadcasted_iota(jnp.int32, (PEERS, BIN_DEV, LANES), 1) == 0
    stage_ref[:, half // LANES * SLOTS :, :] = jnp.where(
        first, labels[:, None, :LANES], labels[:, None, LANES:]
    )

    loads[3].wait()
    count = width // taps
    stacked = jnp.concatenate([traces_ref[:, b * taps : (b + 1) * taps] for b in range(count)], axis=0)
    spread = dot_split(halves(stacked), toeplitz)
    pieces = [
        spread[b * rows : (b + 1) * rows, :taps] + spread[(b - 1) * rows : b * rows, taps:] for b in range(1, count)
    ]
    edge_ref[:, :taps] = spread[:rows, :taps]
    edge_ref[:, taps : 2 * taps] = pieces[0]
    edge_ref[:, 2 * taps : 3 * taps] = pieces[-1]
    edge_ref[:, 3 * taps :] = spread[(count - 1) * rows :, taps:]
    loads[4].wait()
    quarters = [map_ref[:, c * LANES : (c + 1) * LANES] for c in range(half // LANES)]
    place_slots(slot, move_out(jnp.concatenate(pieces, axis=1), quarters), stage_ref, 0)
    body = half // LANES * SLOTS
    start = taps // LANES * SLOTS
    stores = [
        pltpu.make_async_copy(stage_ref.at[:, :body, :], out_hbm.at[:, start : start + body, :], out_sems.at[0]),
        pltpu.make_async_copy(stage_ref.at[:, body:, :], out_hbm.at[:, 2 * body :, :], out_sems.at[1]),
    ]
    for store in stores:
        store.start()
    loads[5].wait()
    loads[6].wait()
    for store in stores:
        store.wait()


def outer_kernel(
    last_ref, before_ref, after_ref, high_ref, low_ref, edge_ref, edge_map_ref, slot_ref, given_hbm,
    out_hbm, stage_ref, out_sems,
):
    rows, taps = before_ref.shape
    body = taps // LANES * SLOTS
    slot = slot_ref[...]
    early = dot_split(halves(before_ref[...]), (high_ref[:, taps:], low_ref[:, taps:])) + edge_ref[:, :taps]
    window = jnp.concatenate([early, edge_ref[:, taps : 2 * taps]], axis=1)
    quarters = [edge_map_ref[:, c * LANES : (c + 1) * LANES] for c in range(taps // LANES)]
    place_slots(slot, move_out(window, quarters), stage_ref, 0)
    first = pltpu.make_async_copy(stage_ref.at[:, :body, :], out_hbm.at[:, :body, :], out_sems.at[0])
    first.start()
    late = dot_split(halves(after_ref[...]), (high_ref[:, :taps], low_ref[:, :taps])) + edge_ref[:, 3 * taps :]
    late = jnp.where(last_ref[0] == 1, 0.0, late)
    window = jnp.concatenate([edge_ref[:, 2 * taps : 3 * taps], late], axis=1)
    quarters = [edge_map_ref[:, taps + c * LANES : taps + (c + 1) * LANES] for c in range(taps // LANES)]
    place_slots(slot, move_out(window, quarters), stage_ref, body)
    second = pltpu.make_async_copy(stage_ref.at[:, body:, :], out_hbm.at[:, 3 * body : 4 * body, :], out_sems.at[1])
    second.start()
    first.wait()
    second.wait()


def combine_kernel(arrived_ref, out_ref):
    parts = out_ref.shape[1] // BIN_DEV - 1
    tile = arrived_ref[0, parts * SLOTS :, :]
    for peer in range(1, PEERS):
        tile = tile + arrived_ref[peer, parts * SLOTS :, :]
    labels = jnp.concatenate([tile[0:1, :], tile[1:2, :]], axis=1)
    shape = (NU * BIN_DEV, PEERS * SLOTS)
    row = lax.broadcasted_iota(jnp.int32, shape, 0)
    column = lax.broadcasted_iota(jnp.int32, shape, 1)
    bin_label = (row % BIN_DEV + 1).astype(jnp.float32)
    hit = (labels == bin_label) & (row // BIN_DEV == column % SLOTS // CAP)
    member = jnp.where(hit, 1.0, 0.0).astype(jnp.bfloat16)
    for c in range(0, parts, 2):
        piece = jnp.concatenate(
            [
                arrived_ref[:, k * SLOTS : (k + 1) * SLOTS, :].reshape(PEERS * SLOTS, LANES)
                for k in (c, c + 1)
            ],
            axis=1,
        )
        high, low = halves(piece)
        total = dot(member, high) + dot(member, low)
        for k in (0, 1):
            out_ref[:, (c + k) * BIN_DEV : (c + k + 1) * BIN_DEV, :] = total[
                :, k * LANES : (k + 1) * LANES
            ].reshape(NU, BIN_DEV, LANES)
    fold = dot(member, jnp.ones((PEERS * SLOTS, LANES), jnp.bfloat16))
    out_ref[:, parts * BIN_DEV :, :] = fold.reshape(NU, BIN_DEV, LANES)


def finish_kernel(arrived_ref, out_ref):
    total = arrived_ref[0]
    for u in range(1, NU):
        total = total + arrived_ref[u]
    parts = total.shape[0] // BIN_DEV - 1
    scale = jnp.sqrt(jnp.maximum(total[parts * BIN_DEV :, :], 1.0))
    for c in range(parts):
        out_ref[:, c * LANES : (c + 1) * LANES] = total[c * BIN_DEV : (c + 1) * BIN_DEV, :] / scale


VMEM = pl.BlockSpec(memory_space=pltpu.VMEM)
SMEM = pl.BlockSpec(memory_space=pltpu.SMEM)
ANY = pl.BlockSpec(memory_space=pl.ANY)
LIMIT = 24 * 1024 * 1024


def f32(*shape):
    return jax.ShapeDtypeStruct(shape, jnp.float32)


def correct_inner(place, traces, sample_map, filters, owner, sub):
    rows, width = traces.shape
    taps = filters.shape[1]
    length = (width // LANES) * SLOTS + BIN_DEV
    return pl.pallas_call(
        inner_kernel,
        out_shape=(
            f32(PEERS, length, LANES),
            jax.ShapeDtypeStruct((taps, 2 * taps), jnp.bfloat16),
            jax.ShapeDtypeStruct((taps, 2 * taps), jnp.bfloat16),
            f32(rows, 4 * taps),
            jax.ShapeDtypeStruct((rows, 2 * taps), jnp.int32),
            jax.ShapeDtypeStruct((1, rows), jnp.int32),
        ),
        in_specs=[SMEM] + [ANY] * 5,
        out_specs=(ANY, VMEM, VMEM, VMEM, VMEM, VMEM),
        scratch_shapes=[
            pltpu.VMEM((rows, width), jnp.float32),
            pltpu.VMEM((rows, width // 2), jnp.int32),
            pltpu.VMEM((1, taps), jnp.float32),
            pltpu.VMEM((1, rows), jnp.int32),
            pltpu.VMEM((1, rows), jnp.int32),
            pltpu.VMEM((PEERS, width // 2 // LANES * SLOTS + BIN_DEV, LANES), jnp.float32),
            pltpu.SemaphoreType.DMA((7,)),
            pltpu.SemaphoreType.DMA((2,)),
        ],
        name="correct_inner",
        cost_estimate=pl.CostEstimate(flops=500_000_000, bytes_accessed=2_000_000, transcendentals=0),
        compiler_params=pltpu.CompilerParams(vmem_limit_bytes=LIMIT),
    )(place, traces, sample_map, filters, owner, sub)


def correct_outer(last, before, after, high, low, edge, edge_map, slot, given):
    taps = before.shape[1]
    return pl.pallas_call(
        outer_kernel,
        out_shape=jax.ShapeDtypeStruct(given.shape, given.dtype),
        in_specs=[SMEM] + [VMEM] * 7 + [ANY],
        out_specs=ANY,
        input_output_aliases={8: 0},
        scratch_shapes=[
            pltpu.VMEM((PEERS, 2 * taps // LANES * SLOTS, LANES), jnp.float32),
            pltpu.SemaphoreType.DMA((2,)),
        ],
        name="correct_outer",
        compiler_params=pltpu.CompilerParams(vmem_limit_bytes=LIMIT),
    )(last, before, after, high, low, edge, edge_map, slot, given)


def on_vmem(kernel, shape, name, operand):
    return pl.pallas_call(
        kernel,
        out_shape=f32(*shape),
        in_specs=[VMEM],
        out_specs=VMEM,
        name=name,
        compiler_params=pltpu.CompilerParams(vmem_limit_bytes=LIMIT),
    )(operand)


def passed_along(value, axis, steps):
    count = lax.axis_size(axis)
    leading, last = (max(0, -steps), min(count, count - steps))
    return lax.ppermute(value, axis, [(source, source + steps) for source in range(leading, last)])


def per_device(traces, filters, owners, sub_bins, sample_map):
    rows, width = traces.shape
    taps = filters.shape[1]
    before = passed_along(traces[:, width - taps :], "section", 1)
    after = passed_along(traces[:, :taps], "section", -1)
    place = lax.axis_index(NEAR).astype(jnp.int32).reshape(1)
    last = (lax.axis_index("section") == lax.axis_size("section") - 1).astype(jnp.int32).reshape(1)
    sent, *kept = correct_inner(
        place, traces, sample_map, filters, owners.reshape(1, rows), sub_bins.reshape(1, rows)
    )
    sent = correct_outer(last, before, after, *kept, sent)
    near = lax.all_to_all(sent, NEAR, split_axis=0, concat_axis=0, tiled=True)
    summed = on_vmem(combine_kernel, (NU, (width // LANES + 1) * BIN_DEV, LANES), "combine", near)
    arrived = lax.all_to_all(summed, "u", split_axis=0, concat_axis=0, tiled=True)
    return on_vmem(finish_kernel, (BIN_DEV, width), "finish", arrived)


def solution(mesh):
    fine = Mesh(mesh.devices.reshape(mesh.devices.shape[0], NY, NU, NW, NC), ("section",) + BINS)
    in_specs = (
        P(BINS, "section"),
        P(BINS, None),
        P(BINS, None),
        P(BINS),
        P(BINS, "section"),
    )
    return jax.shard_map(
        per_device, mesh=fine, in_specs=in_specs, out_specs=P(BINS, "section"), check_vma=False
    )
```

```python
import jax
import jax.numpy as jnp
from jax import lax
from jax.experimental import pallas as pl
from jax.experimental.pallas import tpu as pltpu
from jax.sharding import Mesh
from jax.sharding import PartitionSpec as P

BIN_DEV = 8
CAP = 2
LANES = 128
NY, NU, NW, NC = 4, 8, 2, 2
BINS = ("y", "u", "w", "c")
NEAR = ("y", "w", "c")
PEERS = NY * NW * NC
SLOTS = NU * CAP


def halves(value):
    high = value.astype(jnp.bfloat16)
    low = (value - high.astype(jnp.float32)).astype(jnp.bfloat16)
    return high, low


def dot(a, b):
    return jnp.dot(a, b, preferred_element_type=jnp.float32)


def dot_split(a, b):
    return dot(a[0], b[0]) + (dot(a[1], b[0]) + dot(a[0], b[1]))


def move_out(window, quarters):
    rows, span = window.shape
    step = pltpu.roll(window, span - 1, 1) - window
    lane = lax.broadcasted_iota(jnp.int32, (rows, LANES), 1)
    moved = []
    for c, quarter in enumerate(quarters):
        place = lane + (quarter >> 2)
        weight = (quarter & 3).astype(jnp.float32) * 0.25
        inside = place & (LANES - 1)
        block = place >> 7
        near = slope = None
        for k in range(3):
            columns = slice((c + k) * LANES, (c + k + 1) * LANES)
            value = jnp.take_along_axis(window[:, columns], inside, axis=1, mode="promise_in_bounds")
            change = jnp.take_along_axis(step[:, columns], inside, axis=1, mode="promise_in_bounds")
            near = value if k == 0 else jnp.where(block == k, value, near)
            slope = change if k == 0 else jnp.where(block == k, change, slope)
        moved.append(near + weight * slope)
    return jnp.concatenate(moved, axis=1)


def correct_kernel(
    filter_ref, code_ref, traces_hbm, map_hbm, before_ref, after_ref,
    out_hbm, traces_ref, map_ref, stage_ref, sems, out_sems,
):
    rows, width = traces_ref.shape
    taps = before_ref.shape[1]
    count = width // taps
    loads = []
    for k, (source, target) in enumerate([(traces_hbm, traces_ref), (map_hbm, map_ref)]):
        for half in range(2):
            columns = pl.ds(half * (width // 2), width // 2)
            loads.append(
                pltpu.make_async_copy(source.at[:, columns], target.at[:, columns], sems.at[2 * k + half])
            )
    for load in loads:
        load.start()
    shifted = pltpu.roll(jnp.broadcast_to(filter_ref[...], (taps, 2 * taps)), 0, 1, stride=1, stride_axis=0)
    toeplitz = halves(shifted)

    owner = code_ref[...] // BIN_DEV
    sub = code_ref[...] % BIN_DEV
    owners = NY * NU * NW * NC
    named = lax.broadcasted_iota(jnp.int32, (owners, rows), 0) == owner
    named = jnp.where(named, 1.0, 0.0)
    earlier = lax.broadcasted_iota(jnp.int32, (rows, rows), 0) < lax.broadcasted_iota(jnp.int32, (rows, rows), 1)
    earlier = jnp.where(earlier, 1.0, 0.0).astype(jnp.bfloat16)
    rank = jnp.sum(named * dot(named.astype(jnp.bfloat16), earlier), axis=0, keepdims=True).astype(jnp.int32)
    core, w = owner % NC, owner // NC % NW
    u, y = owner // (NC * NW) % NU, owner // (NC * NW * NU)
    peer = (y * NW + w) * NC + core
    within = u * CAP + rank
    number = lax.broadcasted_iota(jnp.int32, (PEERS * SLOTS, rows), 0)
    member = jnp.where(number == peer * SLOTS + within, 1.0, 0.0).astype(jnp.bfloat16)
    to_peer = lax.broadcasted_iota(jnp.int32, (PEERS, rows), 0) == peer
    to_peer = jnp.where(to_peer, (sub + 1).astype(jnp.float32), 0.0).astype(jnp.bfloat16)
    in_column = jnp.where(number == within + lax.axis_index(NEAR) * SLOTS, 1.0, 0.0).astype(jnp.bfloat16)
    labels = lax.dot_general(to_peer, in_column, (((1,), (1,)), ((), ())), preferred_element_type=jnp.float32)
    first = lax.broadcasted_iota(jnp.int32, (PEERS, BIN_DEV, LANES), 1) == 0
    body = taps // LANES * SLOTS
    stage_ref[:, count * body :, :] = jnp.where(first, labels[:, None, :LANES], labels[:, None, LANES:])

    def store(k, extent):
        part = pl.ds(k * body, extent)
        return pltpu.make_async_copy(stage_ref.at[:, part, :], out_hbm.at[:, part, :], out_sems.at[k])

    stores = [store(count, BIN_DEV)]
    stores[0].start()

    loads[0].wait()
    loads[1].wait()
    stacked = [before_ref[...]] + [traces_ref[:, b * taps : (b + 1) * taps] for b in range(count)] + [after_ref[...]]
    spread = dot_split(halves(jnp.concatenate(stacked, axis=0)), toeplitz)
    pieces = [
        spread[b * rows : (b + 1) * rows, :taps] + spread[(b - 1) * rows : b * rows, taps:]
        for b in range(1, count + 2)
    ]
    pieces[-1] = jnp.where(lax.axis_index("section") == lax.axis_size("section") - 1, 0.0, pieces[-1])
    loads[2].wait()
    loads[3].wait()
    for k in range(count):
        quarters = [map_ref[:, k * taps + c * LANES : k * taps + (c + 1) * LANES] for c in range(taps // LANES)]
        moved = move_out(jnp.concatenate(pieces[k : k + 2], axis=1), quarters)
        high, low = halves(moved)
        placed = dot(member, high) + dot(member, low)
        for c in range(taps // LANES):
            stage_ref[:, k * body + c * SLOTS : k * body + (c + 1) * SLOTS, :] = placed[
                :, c * LANES : (c + 1) * LANES
            ].reshape(PEERS, SLOTS, LANES)
        stores.append(store(k, body))
        stores[-1].start()
    for one in stores:
        one.wait()


def combine_kernel(arrived_ref, out_ref):
    parts = out_ref.shape[1] // BIN_DEV - 1
    tile = arrived_ref[0, parts * SLOTS :, :]
    for peer in range(1, PEERS):
        tile = tile + arrived_ref[peer, parts * SLOTS :, :]
    labels = jnp.concatenate([tile[0:1, :], tile[1:2, :]], axis=1)
    shape = (NU * BIN_DEV, PEERS * SLOTS)
    row = lax.broadcasted_iota(jnp.int32, shape, 0)
    column = lax.broadcasted_iota(jnp.int32, shape, 1)
    bin_label = (row % BIN_DEV + 1).astype(jnp.float32)
    hit = (labels == bin_label) & (row // BIN_DEV == column % SLOTS // CAP)
    member = jnp.where(hit, 1.0, 0.0).astype(jnp.bfloat16)
    for c in range(0, parts, 2):
        piece = jnp.concatenate(
            [
                arrived_ref[:, k * SLOTS : (k + 1) * SLOTS, :].reshape(PEERS * SLOTS, LANES)
                for k in (c, c + 1)
            ],
            axis=1,
        )
        high, low = halves(piece)
        total = dot(member, high) + dot(member, low)
        for k in (0, 1):
            out_ref[:, (c + k) * BIN_DEV : (c + k + 1) * BIN_DEV, :] = total[
                :, k * LANES : (k + 1) * LANES
            ].reshape(NU, BIN_DEV, LANES)
    fold = dot(member, jnp.ones((PEERS * SLOTS, LANES), jnp.bfloat16))
    out_ref[:, parts * BIN_DEV :, :] = fold.reshape(NU, BIN_DEV, LANES)


def finish_kernel(arrived_ref, out_ref):
    total = arrived_ref[0]
    for u in range(1, NU):
        total = total + arrived_ref[u]
    parts = total.shape[0] // BIN_DEV - 1
    scale = jnp.sqrt(jnp.maximum(total[parts * BIN_DEV :, :], 1.0))
    for c in range(parts):
        out_ref[:, c * LANES : (c + 1) * LANES] = total[c * BIN_DEV : (c + 1) * BIN_DEV, :] / scale


VMEM = pl.BlockSpec(memory_space=pltpu.VMEM)
ANY = pl.BlockSpec(memory_space=pl.ANY)
LIMIT = 24 * 1024 * 1024


def f32(*shape):
    return jax.ShapeDtypeStruct(shape, jnp.float32)


def correct(filters, code, traces, sample_map, before, after):
    rows, width = traces.shape
    taps = before.shape[1]
    length = (width // LANES) * SLOTS + BIN_DEV
    return pl.pallas_call(
        correct_kernel,
        out_shape=f32(PEERS, length, LANES),
        in_specs=[VMEM, VMEM, ANY, ANY, VMEM, VMEM],
        out_specs=ANY,
        scratch_shapes=[
            pltpu.VMEM((rows, width), jnp.float32),
            pltpu.VMEM((rows, width), jnp.int32),
            pltpu.VMEM((PEERS, length, LANES), jnp.float32),
            pltpu.SemaphoreType.DMA((4,)),
            pltpu.SemaphoreType.DMA((width // taps + 1,)),
        ],
        name="correct",
        compiler_params=pltpu.CompilerParams(vmem_limit_bytes=55000 * 1024),
    )(filters, code, traces, sample_map, before, after)


def on_vmem(kernel, shape, name, operand):
    return pl.pallas_call(
        kernel,
        out_shape=f32(*shape),
        in_specs=[VMEM],
        out_specs=VMEM,
        name=name,
        compiler_params=pltpu.CompilerParams(vmem_limit_bytes=LIMIT),
    )(operand)


def passed_along(value, axis, steps):
    count = lax.axis_size(axis)
    leading, last = (max(0, -steps), min(count, count - steps))
    return lax.ppermute(value, axis, [(source, source + steps) for source in range(leading, last)])


def per_device(traces, filters, owners, sub_bins, sample_map):
    rows, width = traces.shape
    taps = filters.shape[1]
    before = passed_along(traces[:, width - taps :], "section", 1)
    after = passed_along(traces[:, :taps], "section", -1)
    code = owners.reshape(1, rows) * BIN_DEV + sub_bins.reshape(1, rows)
    padded = jnp.pad(filters, ((0, 0), (0, taps)))
    sent = correct(padded, code, traces, sample_map, before, after)
    near = lax.all_to_all(sent, NEAR, split_axis=0, concat_axis=0, tiled=True)
    summed = on_vmem(combine_kernel, (NU, (width // LANES + 1) * BIN_DEV, LANES), "combine", near)
    arrived = lax.all_to_all(summed, "u", split_axis=0, concat_axis=0, tiled=True)
    return on_vmem(finish_kernel, (BIN_DEV, width), "finish", arrived)


def solution(mesh):
    fine = Mesh(mesh.devices.reshape(mesh.devices.shape[0], NY, NU, NW, NC), ("section",) + BINS)
    in_specs = (
        P(BINS, "section"),
        P(BINS, None),
        P(BINS, None),
        P(BINS),
        P(BINS, "section"),
    )
    return jax.shard_map(
        per_device, mesh=fine, in_specs=in_specs, out_specs=P(BINS, "section"), check_vma=False
    )
```

```python
import jax
import jax.numpy as jnp
from jax import lax
from jax.experimental import pallas as pl
from jax.experimental.pallas import tpu as pltpu
from jax.sharding import Mesh
from jax.sharding import PartitionSpec as P

BIN_DEV = 8
CAP = 2
LANES = 128
NY, NU, NW, NC = 4, 8, 2, 2
BINS = ("y", "u", "w", "c")
NEAR = ("y", "w", "c")
PEERS = NY * NW * NC
SLOTS = NU * CAP
SHELVES = LANES // SLOTS


def halves(value):
    high = value.astype(jnp.bfloat16)
    low = (value - high.astype(jnp.float32)).astype(jnp.bfloat16)
    return high, low


def dot(a, b):
    return jnp.dot(a, b, preferred_element_type=jnp.float32)


def dot_split(a, b):
    return dot(a[0], b[0]) + (dot(a[1], b[0]) + dot(a[0], b[1]))


def move_out(window, quarters):
    rows, span = window.shape
    step = pltpu.roll(window, span - 1, 1) - window
    lane = lax.broadcasted_iota(jnp.int32, (rows, LANES), 1)
    moved = []
    for c, quarter in enumerate(quarters):
        place = lane + (quarter >> 2)
        weight = (quarter & 3).astype(jnp.float32) * 0.25
        inside = place & (LANES - 1)
        block = place >> 7
        near = slope = None
        for k in range(3):
            columns = slice((c + k) * LANES, (c + k + 1) * LANES)
            value = jnp.take_along_axis(window[:, columns], inside, axis=1, mode="promise_in_bounds")
            change = jnp.take_along_axis(step[:, columns], inside, axis=1, mode="promise_in_bounds")
            near = value if k == 0 else jnp.where(block == k, value, near)
            slope = change if k == 0 else jnp.where(block == k, change, slope)
        moved.append(near + weight * slope)
    return jnp.concatenate(moved, axis=1)


def place_slots(slot, moved):
    number = lax.broadcasted_iota(jnp.int32, (PEERS * SLOTS, moved.shape[0]), 0)
    member = jnp.where(number == slot, 1.0, 0.0).astype(jnp.bfloat16)
    high, low = halves(moved)
    return dot(member, high) + dot(member, low)


def inner_kernel(
    filter_ref, code_ref, traces_hbm, map_hbm,
    high_ref, low_ref, edge_ref, edge_map_ref, slot_ref, label_ref, *rest,
):
    *placed_refs, traces_ref, map_ref, sems = rest
    rows, width = traces_ref.shape
    taps = filter_ref.shape[1] // 2
    half = width // 2
    count = width // taps
    loads = []
    for part in range(2):
        columns = pl.ds(part * half, half)
        loads.append(pltpu.make_async_copy(traces_hbm.at[:, columns], traces_ref.at[:, columns], sems.at[part]))
    loads += [
        pltpu.make_async_copy(map_hbm.at[:, taps : taps + half], map_ref, sems.at[2]),
        pltpu.make_async_copy(map_hbm.at[:, :taps], edge_map_ref.at[:, :taps], sems.at[3]),
        pltpu.make_async_copy(map_hbm.at[:, taps + half :], edge_map_ref.at[:, taps:], sems.at[4]),
    ]
    for load in loads:
        load.start()
    shifted = pltpu.roll(jnp.broadcast_to(filter_ref[...], (taps, 2 * taps)), 0, 1, stride=1, stride_axis=0)
    toeplitz = halves(shifted)
    high_ref[...], low_ref[...] = toeplitz

    owner = code_ref[...] // BIN_DEV
    sub = code_ref[...] % BIN_DEV
    owners = NY * NU * NW * NC
    named = lax.broadcasted_iota(jnp.int32, (owners, rows), 0) == owner
    named = jnp.where(named, 1.0, 0.0)
    earlier = lax.broadcasted_iota(jnp.int32, (rows, rows), 0) < lax.broadcasted_iota(jnp.int32, (rows, rows), 1)
    earlier = jnp.where(earlier, 1.0, 0.0).astype(jnp.bfloat16)
    rank = jnp.sum(named * dot(named.astype(jnp.bfloat16), earlier), axis=0, keepdims=True).astype(jnp.int32)
    core, w = owner % NC, owner // NC % NW
    u, y = owner // (NC * NW) % NU, owner // (NC * NW * NU)
    peer = (y * NW + w) * NC + core
    within = u * CAP + rank
    slot = peer * SLOTS + within
    slot_ref[...] = slot
    to_peer = lax.broadcasted_iota(jnp.int32, (PEERS, rows), 0) == peer
    to_peer = jnp.where(to_peer, (sub + 1).astype(jnp.float32), 0.0).astype(jnp.bfloat16)
    column = lax.broadcasted_iota(jnp.int32, (LANES, rows), 0)
    shelf = lax.rem(lax.axis_index(NEAR), SHELVES) * SLOTS
    in_column = jnp.where(column == within + shelf, 1.0, 0.0).astype(jnp.bfloat16)
    label_ref[...] = lax.dot_general(
        to_peer, in_column, (((1,), (1,)), ((), ())), preferred_element_type=jnp.float32
    )

    loads[0].wait()
    loads[1].wait()
    stacked = jnp.concatenate([traces_ref[:, b * taps : (b + 1) * taps] for b in range(count)], axis=0)
    spread = dot_split(halves(stacked), toeplitz)
    pieces = [
        spread[b * rows : (b + 1) * rows, :taps] + spread[(b - 1) * rows : b * rows, taps:] for b in range(1, count)
    ]
    edge_ref[:, :taps] = spread[:rows, :taps]
    edge_ref[:, taps : 2 * taps] = pieces[0]
    edge_ref[:, 2 * taps : 3 * taps] = pieces[-1]
    edge_ref[:, 3 * taps :] = spread[(count - 1) * rows :, taps:]
    loads[2].wait()
    quarters = [map_ref[:, c * LANES : (c + 1) * LANES] for c in range(half // LANES)]
    placed = place_slots(slot, move_out(jnp.concatenate(pieces, axis=1), quarters))
    for c, placed_ref in enumerate(placed_refs):
        placed_ref[...] = placed[:, c * LANES : (c + 1) * LANES]
    loads[3].wait()
    loads[4].wait()


def outer_kernel(before_ref, after_ref, high_ref, low_ref, edge_ref, edge_map_ref, slot_ref, label_ref, *rest):
    *placed_refs, out_ref = rest
    taps = before_ref.shape[1]
    parts = taps // LANES
    length = out_ref.shape[0] // PEERS
    slot = slot_ref[...]

    def put(c, placed):
        for peer in range(PEERS):
            start = peer * length + c * SLOTS
            out_ref[start : start + SLOTS, :] = placed[peer * SLOTS : (peer + 1) * SLOTS, :]

    def put_edge(c, k, window):
        quarters = [edge_map_ref[:, (k + i) * LANES : (k + i + 1) * LANES] for i in range(parts)]
        placed = place_slots(slot, move_out(window, quarters))
        for i in range(parts):
            put(c + i, placed[:, i * LANES : (i + 1) * LANES])

    early = dot_split(halves(before_ref[...]), (high_ref[:, taps:], low_ref[:, taps:])) + edge_ref[:, :taps]
    put_edge(0, 0, jnp.concatenate([early, edge_ref[:, taps : 2 * taps]], axis=1))
    late = dot_split(halves(after_ref[...]), (high_ref[:, :taps], low_ref[:, :taps])) + edge_ref[:, 3 * taps :]
    late = jnp.where(lax.axis_index("section") == lax.axis_size("section") - 1, 0.0, late)
    put_edge(parts + len(placed_refs), parts, jnp.concatenate([edge_ref[:, 2 * taps : 3 * taps], late], axis=1))
    for c, placed_ref in enumerate(placed_refs):
        put(parts + c, placed_ref)
    for peer in range(PEERS):
        out_ref[(peer + 1) * length - 1 : (peer + 1) * length, :] = label_ref[peer : peer + 1, :]


def combine_kernel(arrived_ref, out_ref):
    length = arrived_ref.shape[0] // PEERS
    out_length = out_ref.shape[0] // NU
    parts = length // SLOTS
    shelves = []
    for first in range(0, PEERS, SHELVES):
        row = sum(arrived_ref[(peer + 1) * length - 1 : (peer + 1) * length, :] for peer in range(first, first + SHELVES))
        shelves.append(row)
    labels = jnp.concatenate(shelves, axis=1)
    slots = PEERS * SLOTS
    shape = (NU * BIN_DEV, slots)
    row = lax.broadcasted_iota(jnp.int32, shape, 0)
    column = lax.broadcasted_iota(jnp.int32, shape, 1)
    bin_label = (row % BIN_DEV + 1).astype(jnp.float32)
    hit = (labels == bin_label) & (row // BIN_DEV == column % SLOTS // CAP)
    member = jnp.where(hit, 1.0, 0.0).astype(jnp.bfloat16)
    for c in range(0, parts, 2):
        pair = []
        for k in (c, c + 1):
            starts = [peer * length + k * SLOTS for peer in range(PEERS)]
            pair.append(jnp.concatenate([arrived_ref[start : start + SLOTS, :] for start in starts], axis=0))
        high, low = halves(jnp.concatenate(pair, axis=1))
        total = dot(member, high) + dot(member, low)
        for k in (0, 1):
            for u in range(NU):
                start = u * out_length + (c + k) * BIN_DEV
                out_ref[start : start + BIN_DEV, :] = total[
                    u * BIN_DEV : (u + 1) * BIN_DEV, k * LANES : (k + 1) * LANES
                ]
    column = lax.broadcasted_iota(jnp.int32, (NU, slots), 1)
    of_owner = (lax.broadcasted_iota(jnp.int32, (NU, slots), 0) == column % SLOTS // CAP) & (labels > 0.0)
    of_owner = jnp.where(of_owner, 1.0, 0.0).astype(jnp.bfloat16)
    of_bin = labels == (lax.broadcasted_iota(jnp.int32, (LANES, slots), 0) + 1).astype(jnp.float32)
    of_bin = jnp.where(of_bin, 1.0, 0.0).astype(jnp.bfloat16)
    fold = lax.dot_general(of_owner, of_bin, (((1,), (1,)), ((), ())), preferred_element_type=jnp.float32)
    for u in range(NU):
        out_ref[(u + 1) * out_length - 1 : (u + 1) * out_length, :] = fold[u : u + 1, :]


def finish_kernel(arrived_ref, out_ref):
    length = arrived_ref.shape[0] // NU
    fold = sum(arrived_ref[(u + 1) * length - 1 : (u + 1) * length, :] for u in range(NU))
    diagonal = lax.broadcasted_iota(jnp.int32, (BIN_DEV, LANES), 0) == lax.broadcasted_iota(jnp.int32, (BIN_DEV, LANES), 1)
    counts = jnp.sum(jnp.where(diagonal, fold, 0.0), axis=1, keepdims=True)
    scale = jnp.sqrt(jnp.maximum(counts, 1.0))
    for c in range(length // BIN_DEV):
        starts = [u * length + c * BIN_DEV for u in range(NU)]
        total = sum(arrived_ref[start : start + BIN_DEV, :] for start in starts)
        out_ref[:, c * LANES : (c + 1) * LANES] = total / scale


VMEM = pl.BlockSpec(memory_space=pltpu.VMEM)
ANY = pl.BlockSpec(memory_space=pl.ANY)
LIMIT = 24 * 1024 * 1024
INNER_LIMIT = 53760


def f32(*shape):
    return jax.ShapeDtypeStruct(shape, jnp.float32)


def correct_inner(filters, code, traces, sample_map):
    rows, width = traces.shape
    taps = filters.shape[1] // 2
    inner = (width - 2 * taps) // LANES
    return pl.pallas_call(
        inner_kernel,
        out_shape=(
            jax.ShapeDtypeStruct((taps, 2 * taps), jnp.bfloat16),
            jax.ShapeDtypeStruct((taps, 2 * taps), jnp.bfloat16),
            f32(rows, 4 * taps),
            jax.ShapeDtypeStruct((rows, 2 * taps), jnp.int32),
            jax.ShapeDtypeStruct((1, rows), jnp.int32),
            f32(PEERS, LANES),
        )
        + (f32(PEERS * SLOTS, LANES),) * inner,
        in_specs=[VMEM, VMEM, ANY, ANY],
        out_specs=(VMEM,) * (6 + inner),
        scratch_shapes=[
            pltpu.VMEM((rows, width), jnp.float32),
            pltpu.VMEM((rows, inner * LANES), jnp.int32),
            pltpu.SemaphoreType.DMA((5,)),
        ],
        name="correct_inner",
        cost_estimate=pl.CostEstimate(flops=500_000_000, bytes_accessed=2_000_000, transcendentals=0),
        compiler_params=pltpu.CompilerParams(vmem_limit_bytes=INNER_LIMIT * 1024),
    )(filters, code, traces, sample_map)


def on_vmem(kernel, shape, name, *operands):
    return pl.pallas_call(
        kernel,
        out_shape=f32(*shape),
        in_specs=[VMEM] * len(operands),
        out_specs=VMEM,
        name=name,
        compiler_params=pltpu.CompilerParams(vmem_limit_bytes=LIMIT),
    )(*operands)


def passed_along(value, axis, steps):
    count = lax.axis_size(axis)
    leading, last = (max(0, -steps), min(count, count - steps))
    return lax.ppermute(value, axis, [(source, source + steps) for source in range(leading, last)])


def exchanged(rows, axes):
    count, lanes = rows.shape
    sent = rows.reshape(count, 1, lanes)
    return lax.all_to_all(sent, axes, split_axis=0, concat_axis=0, tiled=True).reshape(count, lanes)


def per_device(traces, filters, owners, sub_bins, sample_map):
    rows, width = traces.shape
    taps = filters.shape[1]
    before = passed_along(traces[:, width - taps :], "section", 1)
    after = passed_along(traces[:, :taps], "section", -1)
    code = owners.reshape(1, rows) * BIN_DEV + sub_bins.reshape(1, rows)
    padded = jnp.pad(filters, ((0, 0), (0, taps)))
    kept = correct_inner(padded, code, traces, sample_map)
    parts = width // LANES
    sent = on_vmem(outer_kernel, (PEERS * (parts * SLOTS + 1), LANES), "correct_outer", before, after, *kept)
    near = exchanged(sent, NEAR)
    summed = on_vmem(combine_kernel, (NU * (parts * BIN_DEV + 1), LANES), "combine", near)
    arrived = exchanged(summed, "u")
    return on_vmem(finish_kernel, (BIN_DEV, width), "finish", arrived)


def solution(mesh):
    fine = Mesh(mesh.devices.reshape(mesh.devices.shape[0], NY, NU, NW, NC), ("section",) + BINS)
    in_specs = (
        P(BINS, "section"),
        P(BINS, None),
        P(BINS, None),
        P(BINS),
        P(BINS, "section"),
    )
    return jax.shard_map(
        per_device, mesh=fine, in_specs=in_specs, out_specs=P(BINS, "section"), check_vma=False
    )
```

```python
import jax
import jax.numpy as jnp
from jax import lax
from jax.experimental import pallas as pl
from jax.experimental.pallas import tpu as pltpu
from jax.sharding import Mesh
from jax.sharding import PartitionSpec as P

BIN_DEV = 8
CAP = 2
LANES = 128
NY, NU, NW, NC = 4, 8, 2, 2
BINS = ("y", "u", "w", "c")
NEAR = ("y", "w", "c")
PEERS = NY * NW * NC
SLOTS = NU * CAP
SHELVES = LANES // SLOTS


def halves(value):
    high = value.astype(jnp.bfloat16)
    low = (value - high.astype(jnp.float32)).astype(jnp.bfloat16)
    return high, low


def dot(a, b):
    return jnp.dot(a, b, preferred_element_type=jnp.float32)


def dot_split(a, b):
    return dot(a[0], b[0]) + (dot(a[1], b[0]) + dot(a[0], b[1]))


def move_out(window, quarters):
    rows, span = window.shape
    step = pltpu.roll(window, span - 1, 1) - window
    lane = lax.broadcasted_iota(jnp.int32, (rows, LANES), 1)
    moved = []
    for c, quarter in enumerate(quarters):
        place = lane + (quarter >> 2)
        weight = (quarter & 3).astype(jnp.float32) * 0.25
        inside = place & (LANES - 1)
        block = place >> 7
        near = slope = None
        for k in range(3):
            columns = slice((c + k) * LANES, (c + k + 1) * LANES)
            value = jnp.take_along_axis(window[:, columns], inside, axis=1, mode="promise_in_bounds")
            change = jnp.take_along_axis(step[:, columns], inside, axis=1, mode="promise_in_bounds")
            near = value if k == 0 else jnp.where(block == k, value, near)
            slope = change if k == 0 else jnp.where(block == k, change, slope)
        moved.append(near + weight * slope)
    return jnp.concatenate(moved, axis=1)


def place_slots(slot, moved):
    number = lax.broadcasted_iota(jnp.int32, (PEERS * SLOTS, moved.shape[0]), 0)
    member = jnp.where(number == slot, 1.0, 0.0).astype(jnp.bfloat16)
    high, low = halves(moved)
    return dot(member, high) + dot(member, low)


def inner_kernel(
    small_ref, traces_hbm, map_hbm,
    high_ref, low_ref, edge_ref, edge_map_ref, slot_ref, label_ref, *rest,
):
    *placed_refs, traces_ref, map_ref, sems = rest
    rows, width = traces_ref.shape
    taps = (small_ref.shape[1] - LANES) // 2
    half = width // 2
    count = width // taps
    loads = []
    for part in range(2):
        columns = pl.ds(part * half, half)
        loads.append(pltpu.make_async_copy(traces_hbm.at[:, columns], traces_ref.at[:, columns], sems.at[part]))
    loads += [
        pltpu.make_async_copy(map_hbm.at[:, taps : taps + half], map_ref, sems.at[2]),
        pltpu.make_async_copy(map_hbm.at[:, :taps], edge_map_ref.at[:, :taps], sems.at[3]),
        pltpu.make_async_copy(map_hbm.at[:, taps + half :], edge_map_ref.at[:, taps:], sems.at[4]),
    ]
    for load in loads:
        load.start()
    shifted = pltpu.roll(jnp.broadcast_to(small_ref[:, : 2 * taps], (taps, 2 * taps)), 0, 1, stride=1, stride_axis=0)
    toeplitz = halves(shifted)
    high_ref[...], low_ref[...] = toeplitz

    code = small_ref[:, 2 * taps : 2 * taps + rows].astype(jnp.int32)
    owner, sub = code // BIN_DEV, code % BIN_DEV
    owners = NY * NU * NW * NC
    named = lax.broadcasted_iota(jnp.int32, (owners, rows), 0) == owner
    named = jnp.where(named, 1.0, 0.0)
    earlier = lax.broadcasted_iota(jnp.int32, (rows, rows), 0) < lax.broadcasted_iota(jnp.int32, (rows, rows), 1)
    earlier = jnp.where(earlier, 1.0, 0.0).astype(jnp.bfloat16)
    rank = jnp.sum(named * dot(named.astype(jnp.bfloat16), earlier), axis=0, keepdims=True).astype(jnp.int32)
    core, w = owner % NC, owner // NC % NW
    u, y = owner // (NC * NW) % NU, owner // (NC * NW * NU)
    peer = (y * NW + w) * NC + core
    within = u * CAP + rank
    slot = peer * SLOTS + within
    slot_ref[...] = slot
    to_peer = lax.broadcasted_iota(jnp.int32, (PEERS, rows), 0) == peer
    to_peer = jnp.where(to_peer, (sub + 1).astype(jnp.float32), 0.0).astype(jnp.bfloat16)
    column = lax.broadcasted_iota(jnp.int32, (LANES, rows), 0)
    shelf = lax.rem(lax.axis_index(NEAR), SHELVES) * SLOTS
    in_column = jnp.where(column == within + shelf, 1.0, 0.0).astype(jnp.bfloat16)
    label_ref[...] = lax.dot_general(
        to_peer, in_column, (((1,), (1,)), ((), ())), preferred_element_type=jnp.float32
    )

    loads[0].wait()
    loads[1].wait()
    stacked = jnp.concatenate([traces_ref[:, b * taps : (b + 1) * taps] for b in range(count)], axis=0)
    spread = dot_split(halves(stacked), toeplitz)
    pieces = [
        spread[b * rows : (b + 1) * rows, :taps] + spread[(b - 1) * rows : b * rows, taps:] for b in range(1, count)
    ]
    edge_ref[:, :taps] = spread[:rows, :taps]
    edge_ref[:, taps : 2 * taps] = pieces[0]
    edge_ref[:, 2 * taps : 3 * taps] = pieces[-1]
    edge_ref[:, 3 * taps :] = spread[(count - 1) * rows :, taps:]
    loads[2].wait()
    quarters = [map_ref[:, c * LANES : (c + 1) * LANES] for c in range(half // LANES)]
    placed = place_slots(slot, move_out(jnp.concatenate(pieces, axis=1), quarters))
    for c, placed_ref in enumerate(placed_refs):
        placed_ref[...] = placed[:, c * LANES : (c + 1) * LANES]
    loads[3].wait()
    loads[4].wait()


def outer_kernel(pair_ref, cross_ref, high_ref, low_ref, edge_ref, edge_map_ref, slot_ref, label_ref, *rest):
    *placed_refs, out_ref = rest
    taps = pair_ref.shape[1]
    parts = taps // LANES
    length = out_ref.shape[0] // PEERS
    slot = slot_ref[...]

    def put(c, placed):
        for peer in range(PEERS):
            start = peer * length + c * SLOTS
            out_ref[start : start + SLOTS, :] = placed[peer * SLOTS : (peer + 1) * SLOTS, :]

    def put_edge(c, k, window):
        quarters = [edge_map_ref[:, (k + i) * LANES : (k + i + 1) * LANES] for i in range(parts)]
        placed = place_slots(slot, move_out(window, quarters))
        for i in range(parts):
            put(c + i, placed[:, i * LANES : (i + 1) * LANES])

    place = lax.axis_index("section")
    odd = lax.rem(place, 2) == 1
    pair, cross = pair_ref[...], cross_ref[...]
    before, after = jnp.where(odd, pair, cross), jnp.where(odd, cross, pair)
    early = dot_split(halves(before), (high_ref[:, taps:], low_ref[:, taps:])) + edge_ref[:, :taps]
    put_edge(0, 0, jnp.concatenate([early, edge_ref[:, taps : 2 * taps]], axis=1))
    late = dot_split(halves(after), (high_ref[:, :taps], low_ref[:, :taps])) + edge_ref[:, 3 * taps :]
    late = jnp.where(place == lax.axis_size("section") - 1, 0.0, late)
    put_edge(parts + len(placed_refs), parts, jnp.concatenate([edge_ref[:, 2 * taps : 3 * taps], late], axis=1))
    for c, placed_ref in enumerate(placed_refs):
        put(parts + c, placed_ref)
    for peer in range(PEERS):
        out_ref[(peer + 1) * length - 1 : (peer + 1) * length, :] = label_ref[peer : peer + 1, :]


def combine_kernel(arrived_ref, out_ref):
    length = arrived_ref.shape[0] // PEERS
    out_length = out_ref.shape[0] // NU
    parts = length // SLOTS
    shelves = []
    for first in range(0, PEERS, SHELVES):
        row = sum(arrived_ref[(peer + 1) * length - 1 : (peer + 1) * length, :] for peer in range(first, first + SHELVES))
        shelves.append(row)
    labels = jnp.concatenate(shelves, axis=1)
    slots = PEERS * SLOTS
    shape = (NU * BIN_DEV, slots)
    row = lax.broadcasted_iota(jnp.int32, shape, 0)
    column = lax.broadcasted_iota(jnp.int32, shape, 1)
    bin_label = (row % BIN_DEV + 1).astype(jnp.float32)
    hit = (labels == bin_label) & (row // BIN_DEV == column % SLOTS // CAP)
    member = jnp.where(hit, 1.0, 0.0).astype(jnp.bfloat16)
    for c in range(0, parts, 2):
        pair = []
        for k in (c, c + 1):
            starts = [peer * length + k * SLOTS for peer in range(PEERS)]
            pair.append(jnp.concatenate([arrived_ref[start : start + SLOTS, :] for start in starts], axis=0))
        high, low = halves(jnp.concatenate(pair, axis=1))
        total = dot(member, high) + dot(member, low)
        for k in (0, 1):
            for u in range(NU):
                start = u * out_length + (c + k) * BIN_DEV
                out_ref[start : start + BIN_DEV, :] = total[
                    u * BIN_DEV : (u + 1) * BIN_DEV, k * LANES : (k + 1) * LANES
                ]
    column = lax.broadcasted_iota(jnp.int32, (NU, slots), 1)
    of_owner = (lax.broadcasted_iota(jnp.int32, (NU, slots), 0) == column % SLOTS // CAP) & (labels > 0.0)
    of_owner = jnp.where(of_owner, 1.0, 0.0).astype(jnp.bfloat16)
    of_bin = labels == (lax.broadcasted_iota(jnp.int32, (LANES, slots), 0) + 1).astype(jnp.float32)
    of_bin = jnp.where(of_bin, 1.0, 0.0).astype(jnp.bfloat16)
    fold = lax.dot_general(of_owner, of_bin, (((1,), (1,)), ((), ())), preferred_element_type=jnp.float32)
    for u in range(NU):
        out_ref[(u + 1) * out_length - 1 : (u + 1) * out_length, :] = fold[u : u + 1, :]


def finish_kernel(arrived_ref, out_ref):
    length = arrived_ref.shape[0] // NU
    fold = sum(arrived_ref[(u + 1) * length - 1 : (u + 1) * length, :] for u in range(NU))
    diagonal = lax.broadcasted_iota(jnp.int32, (BIN_DEV, LANES), 0) == lax.broadcasted_iota(jnp.int32, (BIN_DEV, LANES), 1)
    counts = jnp.sum(jnp.where(diagonal, fold, 0.0), axis=1, keepdims=True)
    scale = jnp.sqrt(jnp.maximum(counts, 1.0))
    for c in range(length // BIN_DEV):
        starts = [u * length + c * BIN_DEV for u in range(NU)]
        total = sum(arrived_ref[start : start + BIN_DEV, :] for start in starts)
        out_ref[:, c * LANES : (c + 1) * LANES] = total / scale


VMEM = pl.BlockSpec(memory_space=pltpu.VMEM)
ANY = pl.BlockSpec(memory_space=pl.ANY)
LIMIT = 24 * 1024 * 1024
INNER_LIMIT = 53760


def f32(*shape):
    return jax.ShapeDtypeStruct(shape, jnp.float32)


def correct_inner(small, traces, sample_map):
    rows, width = traces.shape
    taps = (small.shape[1] - LANES) // 2
    inner = (width - 2 * taps) // LANES
    return pl.pallas_call(
        inner_kernel,
        out_shape=(
            jax.ShapeDtypeStruct((taps, 2 * taps), jnp.bfloat16),
            jax.ShapeDtypeStruct((taps, 2 * taps), jnp.bfloat16),
            f32(rows, 4 * taps),
            jax.ShapeDtypeStruct((rows, 2 * taps), jnp.int32),
            jax.ShapeDtypeStruct((1, rows), jnp.int32),
            f32(PEERS, LANES),
        )
        + (f32(PEERS * SLOTS, LANES),) * inner,
        in_specs=[VMEM, ANY, ANY],
        out_specs=(VMEM,) * (6 + inner),
        scratch_shapes=[
            pltpu.VMEM((rows, width), jnp.float32),
            pltpu.VMEM((rows, inner * LANES), jnp.int32),
            pltpu.SemaphoreType.DMA((5,)),
        ],
        name="correct_inner",
        cost_estimate=pl.CostEstimate(flops=500_000_000, bytes_accessed=2_000_000, transcendentals=0),
        compiler_params=pltpu.CompilerParams(vmem_limit_bytes=INNER_LIMIT * 1024),
    )(small, traces, sample_map)


def on_vmem(kernel, shape, name, *operands):
    return pl.pallas_call(
        kernel,
        out_shape=f32(*shape),
        in_specs=[VMEM] * len(operands),
        out_specs=VMEM,
        name=name,
        compiler_params=pltpu.CompilerParams(vmem_limit_bytes=LIMIT),
    )(*operands)


def swapped(value, axis, first):
    count = lax.axis_size(axis)
    pairs = [(one, one + 1) for one in range(first, count - 1, 2)]
    return lax.ppermute(value, axis, pairs + [(other, one) for one, other in pairs])


def exchanged(rows, axes):
    count, lanes = rows.shape
    sent = rows.reshape(count, 1, lanes)
    return lax.all_to_all(sent, axes, split_axis=0, concat_axis=0, tiled=True).reshape(count, lanes)


def per_device(traces, filters, owners, sub_bins, sample_map):
    rows, width = traces.shape
    taps = filters.shape[1]
    odd = lax.axis_index("section") % 2
    ends = [lax.dynamic_slice_in_dim(traces, (width - taps) * use_tail, taps, 1) for use_tail in (1 - odd, odd)]
    pair, cross = swapped(ends[0], "section", 0), swapped(ends[1], "section", 1)
    code = (owners.reshape(1, rows) * BIN_DEV + sub_bins.reshape(1, rows)).astype(jnp.float32)
    small = jnp.pad(filters, ((0, 0), (0, taps + LANES))) + jnp.pad(code, ((0, 0), (2 * taps, LANES - rows)))
    kept = correct_inner(small, traces, sample_map)
    parts = width // LANES
    sent = on_vmem(outer_kernel, (PEERS * (parts * SLOTS + 1), LANES), "correct_outer", pair, cross, *kept)
    near = exchanged(sent, NEAR)
    summed = on_vmem(combine_kernel, (NU * (parts * BIN_DEV + 1), LANES), "combine", near)
    arrived = exchanged(summed, "u")
    return on_vmem(finish_kernel, (BIN_DEV, width), "finish", arrived)


def solution(mesh):
    fine = Mesh(mesh.devices.reshape(mesh.devices.shape[0], NY, NU, NW, NC), ("section",) + BINS)
    in_specs = (
        P(BINS, "section"),
        P(BINS, None),
        P(BINS, None),
        P(BINS),
        P(BINS, "section"),
    )
    return jax.shard_map(
        per_device, mesh=fine, in_specs=in_specs, out_specs=P(BINS, "section"), check_vma=False
    )
```

```python
import jax
import jax.numpy as jnp
from jax import lax
from jax.experimental import pallas as pl
from jax.experimental.pallas import tpu as pltpu
from jax.sharding import Mesh
from jax.sharding import PartitionSpec as P

BIN_DEV = 8
CAP = 2
LANES = 128
NY, NU, NW, NC = 4, 8, 2, 2
BINS = ("y", "u", "w", "c")
NEAR = ("y", "w", "c")
PEERS = NY * NW * NC
SLOTS = NU * CAP
SHELVES = LANES // SLOTS


def halves(value):
    high = value.astype(jnp.bfloat16)
    low = (value - high.astype(jnp.float32)).astype(jnp.bfloat16)
    return high, low


def dot(a, b):
    return jnp.dot(a, b, preferred_element_type=jnp.float32)


def dot_split(a, b):
    return dot(jnp.concatenate([a[0], a[1], a[0]], axis=1), jnp.concatenate([b[0], b[0], b[1]], axis=0))


def dot_exact(member, value):
    return dot(jnp.concatenate([member, member], axis=1), jnp.concatenate(halves(value), axis=0))


def move_out(window, quarters):
    rows, span = window.shape
    step = pltpu.roll(window, span - 1, 1) - window
    lane = lax.broadcasted_iota(jnp.int32, (rows, LANES), 1)
    moved = []
    for c, quarter in enumerate(quarters):
        place = lane + (quarter >> 2)
        weight = (quarter & 3).astype(jnp.float32) * 0.25
        inside = place & (LANES - 1)
        block = place >> 7
        near = slope = None
        for k in range(3):
            columns = slice((c + k) * LANES, (c + k + 1) * LANES)
            value = jnp.take_along_axis(window[:, columns], inside, axis=1, mode="promise_in_bounds")
            change = jnp.take_along_axis(step[:, columns], inside, axis=1, mode="promise_in_bounds")
            near = value if k == 0 else jnp.where(block == k, value, near)
            slope = change if k == 0 else jnp.where(block == k, change, slope)
        moved.append(near + weight * slope)
    return jnp.concatenate(moved, axis=1)


def place_slots(slot, moved):
    number = lax.broadcasted_iota(jnp.int32, (PEERS * SLOTS, moved.shape[0]), 0)
    member = jnp.where(number == slot, 1.0, 0.0).astype(jnp.bfloat16)
    return dot_exact(member, moved)


def inner_kernel(
    small_ref, traces_hbm, map_hbm,
    high_ref, low_ref, edge_ref, edge_map_ref, slot_ref, label_ref, *rest,
):
    *placed_refs, traces_ref, map_ref, sems = rest
    rows, width = traces_ref.shape
    taps = (small_ref.shape[1] - LANES) // 2
    half = width // 2
    count = width // taps
    loads = []
    for part in range(2):
        columns = pl.ds(part * half, half)
        loads.append(pltpu.make_async_copy(traces_hbm.at[:, columns], traces_ref.at[:, columns], sems.at[part]))
    loads += [
        pltpu.make_async_copy(map_hbm.at[:, taps : taps + half], map_ref, sems.at[2]),
        pltpu.make_async_copy(map_hbm.at[:, :taps], edge_map_ref.at[:, :taps], sems.at[3]),
        pltpu.make_async_copy(map_hbm.at[:, taps + half :], edge_map_ref.at[:, taps:], sems.at[4]),
    ]
    for load in loads:
        load.start()
    shifted = pltpu.roll(jnp.broadcast_to(small_ref[:, : 2 * taps], (taps, 2 * taps)), 0, 1, stride=1, stride_axis=0)
    toeplitz = halves(shifted)
    high_ref[...], low_ref[...] = toeplitz

    code = small_ref[:, 2 * taps : 2 * taps + rows].astype(jnp.int32)
    owner, sub = code // BIN_DEV, code % BIN_DEV
    owners = NY * NU * NW * NC
    named = lax.broadcasted_iota(jnp.int32, (owners, rows), 0) == owner
    named = jnp.where(named, 1.0, 0.0)
    earlier = lax.broadcasted_iota(jnp.int32, (rows, rows), 0) < lax.broadcasted_iota(jnp.int32, (rows, rows), 1)
    earlier = jnp.where(earlier, 1.0, 0.0).astype(jnp.bfloat16)
    rank = jnp.sum(named * dot(named.astype(jnp.bfloat16), earlier), axis=0, keepdims=True).astype(jnp.int32)
    core, w = owner % NC, owner // NC % NW
    u, y = owner // (NC * NW) % NU, owner // (NC * NW * NU)
    peer = (y * NW + w) * NC + core
    within = u * CAP + rank
    slot = peer * SLOTS + within
    slot_ref[...] = slot
    to_peer = lax.broadcasted_iota(jnp.int32, (PEERS, rows), 0) == peer
    to_peer = jnp.where(to_peer, (sub + 1).astype(jnp.float32), 0.0).astype(jnp.bfloat16)
    column = lax.broadcasted_iota(jnp.int32, (LANES, rows), 0)
    shelf = lax.rem(lax.axis_index(NEAR), SHELVES) * SLOTS
    in_column = jnp.where(column == within + shelf, 1.0, 0.0).astype(jnp.bfloat16)
    label_ref[...] = lax.dot_general(
        to_peer, in_column, (((1,), (1,)), ((), ())), preferred_element_type=jnp.float32
    )

    loads[0].wait()
    loads[1].wait()
    stacked = jnp.concatenate([traces_ref[:, b * taps : (b + 1) * taps] for b in range(count)], axis=0)
    spread = dot_split(halves(stacked), toeplitz)
    pieces = [
        spread[b * rows : (b + 1) * rows, :taps] + spread[(b - 1) * rows : b * rows, taps:] for b in range(1, count)
    ]
    edge_ref[:, :taps] = spread[:rows, :taps]
    edge_ref[:, taps : 2 * taps] = pieces[0]
    edge_ref[:, 2 * taps : 3 * taps] = pieces[-1]
    edge_ref[:, 3 * taps :] = spread[(count - 1) * rows :, taps:]
    loads[2].wait()
    quarters = [map_ref[:, c * LANES : (c + 1) * LANES] for c in range(half // LANES)]
    placed = place_slots(slot, move_out(jnp.concatenate(pieces, axis=1), quarters))
    for c, placed_ref in enumerate(placed_refs):
        placed_ref[...] = placed[:, c * LANES : (c + 1) * LANES]
    loads[3].wait()
    loads[4].wait()


def outer_kernel(cross_ref, pair_ref, high_ref, low_ref, edge_ref, edge_map_ref, slot_ref, label_ref, *rest):
    *placed_refs, out_ref = rest
    taps = pair_ref.shape[1]
    parts = taps // LANES
    length = out_ref.shape[0] // PEERS
    slot = slot_ref[...]

    def put(c, placed):
        for peer in range(PEERS):
            start = peer * length + c * SLOTS
            out_ref[start : start + SLOTS, :] = placed[peer * SLOTS : (peer + 1) * SLOTS, :]

    def put_edge(c, k, window):
        quarters = [edge_map_ref[:, (k + i) * LANES : (k + i + 1) * LANES] for i in range(parts)]
        placed = place_slots(slot, move_out(window, quarters))
        for i in range(parts):
            put(c + i, placed[:, i * LANES : (i + 1) * LANES])

    place = lax.axis_index("section")
    odd = lax.rem(place, 2) == 1
    pair, cross = pair_ref[...], cross_ref[...]
    before, after = jnp.where(odd, pair, cross), jnp.where(odd, cross, pair)
    early = dot_split(halves(before), (high_ref[:, taps:], low_ref[:, taps:])) + edge_ref[:, :taps]
    put_edge(0, 0, jnp.concatenate([early, edge_ref[:, taps : 2 * taps]], axis=1))
    late = dot_split(halves(after), (high_ref[:, :taps], low_ref[:, :taps])) + edge_ref[:, 3 * taps :]
    late = jnp.where(place == lax.axis_size("section") - 1, 0.0, late)
    put_edge(parts + len(placed_refs), parts, jnp.concatenate([edge_ref[:, 2 * taps : 3 * taps], late], axis=1))
    for c, placed_ref in enumerate(placed_refs):
        put(parts + c, placed_ref)
    for peer in range(PEERS):
        out_ref[(peer + 1) * length - 1 : (peer + 1) * length, :] = label_ref[peer : peer + 1, :]


def combine_kernel(arrived_ref, out_ref):
    length = arrived_ref.shape[0] // PEERS
    out_length = out_ref.shape[0] // NU
    parts = length // SLOTS
    shelves = []
    for first in range(0, PEERS, SHELVES):
        row = sum(arrived_ref[(peer + 1) * length - 1 : (peer + 1) * length, :] for peer in range(first, first + SHELVES))
        shelves.append(row)
    labels = jnp.concatenate(shelves, axis=1)
    slots = PEERS * SLOTS
    shape = (NU * BIN_DEV, slots)
    row = lax.broadcasted_iota(jnp.int32, shape, 0)
    column = lax.broadcasted_iota(jnp.int32, shape, 1)
    bin_label = (row % BIN_DEV + 1).astype(jnp.float32)
    hit = (labels == bin_label) & (row // BIN_DEV == column % SLOTS // CAP)
    member = jnp.where(hit, 1.0, 0.0).astype(jnp.bfloat16)
    for c in range(0, parts, 2):
        pair = []
        for k in (c, c + 1):
            starts = [peer * length + k * SLOTS for peer in range(PEERS)]
            pair.append(jnp.concatenate([arrived_ref[start : start + SLOTS, :] for start in starts], axis=0))
        total = dot_exact(member, jnp.concatenate(pair, axis=1))
        for k in (0, 1):
            for u in range(NU):
                start = u * out_length + (c + k) * BIN_DEV
                out_ref[start : start + BIN_DEV, :] = total[
                    u * BIN_DEV : (u + 1) * BIN_DEV, k * LANES : (k + 1) * LANES
                ]
    column = lax.broadcasted_iota(jnp.int32, (NU, slots), 1)
    of_owner = (lax.broadcasted_iota(jnp.int32, (NU, slots), 0) == column % SLOTS // CAP) & (labels > 0.0)
    of_owner = jnp.where(of_owner, 1.0, 0.0).astype(jnp.bfloat16)
    of_bin = labels == (lax.broadcasted_iota(jnp.int32, (LANES, slots), 0) + 1).astype(jnp.float32)
    of_bin = jnp.where(of_bin, 1.0, 0.0).astype(jnp.bfloat16)
    fold = lax.dot_general(of_owner, of_bin, (((1,), (1,)), ((), ())), preferred_element_type=jnp.float32)
    for u in range(NU):
        out_ref[(u + 1) * out_length - 1 : (u + 1) * out_length, :] = fold[u : u + 1, :]


def finish_kernel(arrived_ref, out_ref):
    length = arrived_ref.shape[0] // NU
    fold = sum(arrived_ref[(u + 1) * length - 1 : (u + 1) * length, :] for u in range(NU))
    diagonal = lax.broadcasted_iota(jnp.int32, (BIN_DEV, LANES), 0) == lax.broadcasted_iota(jnp.int32, (BIN_DEV, LANES), 1)
    counts = jnp.sum(jnp.where(diagonal, fold, 0.0), axis=1, keepdims=True)
    scale = jnp.sqrt(jnp.maximum(counts, 1.0))
    for c in range(length // BIN_DEV):
        starts = [u * length + c * BIN_DEV for u in range(NU)]
        total = sum(arrived_ref[start : start + BIN_DEV, :] for start in starts)
        out_ref[:, c * LANES : (c + 1) * LANES] = total / scale


VMEM = pl.BlockSpec(memory_space=pltpu.VMEM)
ANY = pl.BlockSpec(memory_space=pl.ANY)
LIMIT = 24 * 1024 * 1024
INNER_LIMIT = 53760


def f32(*shape):
    return jax.ShapeDtypeStruct(shape, jnp.float32)


def correct_inner(small, traces, sample_map):
    rows, width = traces.shape
    taps = (small.shape[1] - LANES) // 2
    inner = (width - 2 * taps) // LANES
    return pl.pallas_call(
        inner_kernel,
        out_shape=(
            jax.ShapeDtypeStruct((taps, 2 * taps), jnp.bfloat16),
            jax.ShapeDtypeStruct((taps, 2 * taps), jnp.bfloat16),
            f32(rows, 4 * taps),
            jax.ShapeDtypeStruct((rows, 2 * taps), jnp.int32),
            jax.ShapeDtypeStruct((1, rows), jnp.int32),
            f32(PEERS, LANES),
        )
        + (f32(PEERS * SLOTS, LANES),) * inner,
        in_specs=[VMEM, ANY, ANY],
        out_specs=(VMEM,) * (6 + inner),
        scratch_shapes=[
            pltpu.VMEM((rows, width), jnp.float32),
            pltpu.VMEM((rows, inner * LANES), jnp.int32),
            pltpu.SemaphoreType.DMA((5,)),
        ],
        name="correct_inner",
        cost_estimate=pl.CostEstimate(flops=500_000_000, bytes_accessed=2_000_000, transcendentals=0),
        compiler_params=pltpu.CompilerParams(vmem_limit_bytes=INNER_LIMIT * 1024),
    )(small, traces, sample_map)


def on_vmem(kernel, shape, name, *operands):
    return pl.pallas_call(
        kernel,
        out_shape=f32(*shape),
        in_specs=[VMEM] * len(operands),
        out_specs=VMEM,
        name=name,
        compiler_params=pltpu.CompilerParams(vmem_limit_bytes=LIMIT),
    )(*operands)


def swapped(value, axis, first):
    count = lax.axis_size(axis)
    pairs = [(one, one + 1) for one in range(first, count - 1, 2)]
    return lax.ppermute(value, axis, pairs + [(other, one) for one, other in pairs])


def exchanged(rows, axes):
    count, lanes = rows.shape
    sent = rows.reshape(count, 1, lanes)
    return lax.all_to_all(sent, axes, split_axis=0, concat_axis=0, tiled=True).reshape(count, lanes)


def per_device(traces, filters, owners, sub_bins, sample_map):
    rows, width = traces.shape
    taps = filters.shape[1]
    odd = lax.axis_index("section") % 2
    ends = [lax.dynamic_slice_in_dim(traces, (width - taps) * use_tail, taps, 1) for use_tail in (1 - odd, odd)]
    cross = swapped(ends[1], "section", 1)
    pair = swapped(ends[0], "section", 0)
    code = (owners.reshape(1, rows) * BIN_DEV + sub_bins.reshape(1, rows)).astype(jnp.float32)
    small = jnp.pad(filters, ((0, 0), (0, taps + LANES))) + jnp.pad(code, ((0, 0), (2 * taps, LANES - rows)))
    kept = correct_inner(small, traces, sample_map)
    parts = width // LANES
    sent = on_vmem(outer_kernel, (PEERS * (parts * SLOTS + 1), LANES), "correct_outer", cross, pair, *kept)
    near = exchanged(sent, NEAR)
    summed = on_vmem(combine_kernel, (NU * (parts * BIN_DEV + 1), LANES), "combine", near)
    arrived = exchanged(summed, "u")
    return on_vmem(finish_kernel, (BIN_DEV, width), "finish", arrived)


def solution(mesh):
    fine = Mesh(mesh.devices.reshape(mesh.devices.shape[0], NY, NU, NW, NC), ("section",) + BINS)
    in_specs = (
        P(BINS, "section"),
        P(BINS, None),
        P(BINS, None),
        P(BINS),
        P(BINS, "section"),
    )
    return jax.shard_map(
        per_device, mesh=fine, in_specs=in_specs, out_specs=P(BINS, "section"), check_vma=False
    )
```

```python
import jax
import jax.numpy as jnp
from jax import lax
from jax.experimental import pallas as pl
from jax.experimental.pallas import tpu as pltpu
from jax.sharding import Mesh
from jax.sharding import PartitionSpec as P

BIN_DEV = 8
CAP = 2
LANES = 128
NY, NU, NW, NC = 4, 8, 2, 2
BINS = ("y", "u", "w", "c")
NEAR = ("y", "w", "c")
PEERS = NY * NW * NC
SLOTS = NU * CAP
SHELVES = LANES // SLOTS


def halves(value):
    high = value.astype(jnp.bfloat16)
    low = (value - high.astype(jnp.float32)).astype(jnp.bfloat16)
    return high, low


def dot(a, b):
    return jnp.dot(a, b, preferred_element_type=jnp.float32)


def dot_split(a, b):
    return dot(jnp.concatenate([a[0], a[1], a[0]], axis=1), jnp.concatenate([b[0], b[0], b[1]], axis=0))


def dot_exact(member, value):
    return dot(jnp.concatenate([member, member], axis=1), jnp.concatenate(halves(value), axis=0))


def move_out(window, quarters):
    rows, span = window.shape
    step = pltpu.roll(window, span - 1, 1) - window
    lane = lax.broadcasted_iota(jnp.int32, (rows, LANES), 1)
    moved = []
    for c, quarter in enumerate(quarters):
        place = lane + (quarter >> 2)
        weight = (quarter & 3).astype(jnp.float32) * 0.25
        inside = place & (LANES - 1)
        block = place >> 7
        near = slope = None
        for k in range(3):
            columns = slice((c + k) * LANES, (c + k + 1) * LANES)
            value = jnp.take_along_axis(window[:, columns], inside, axis=1, mode="promise_in_bounds")
            change = jnp.take_along_axis(step[:, columns], inside, axis=1, mode="promise_in_bounds")
            near = value if k == 0 else jnp.where(block == k, value, near)
            slope = change if k == 0 else jnp.where(block == k, change, slope)
        moved.append(near + weight * slope)
    return jnp.concatenate(moved, axis=1)


def place_slots(slot, moved):
    number = lax.broadcasted_iota(jnp.int32, (PEERS * SLOTS, moved.shape[0]), 0)
    member = jnp.where(number == slot, 1.0, 0.0).astype(jnp.bfloat16)
    return dot_exact(member, moved)


def inner_kernel(
    small_ref, traces_hbm, map_hbm,
    high_ref, low_ref, edge_ref, edge_map_ref, slot_ref, label_ref, *rest,
):
    *placed_refs, traces_ref, map_ref, sems = rest
    rows, width = traces_ref.shape
    taps = (small_ref.shape[1] - LANES) // 2
    half = width // 2
    count = width // taps
    loads = []
    for part in range(2):
        columns = pl.ds(part * half, half)
        loads.append(pltpu.make_async_copy(traces_hbm.at[:, columns], traces_ref.at[:, columns], sems.at[part]))
    loads += [
        pltpu.make_async_copy(map_hbm.at[:, taps : taps + half], map_ref, sems.at[2]),
        pltpu.make_async_copy(map_hbm.at[:, :taps], edge_map_ref.at[:, :taps], sems.at[3]),
        pltpu.make_async_copy(map_hbm.at[:, taps + half :], edge_map_ref.at[:, taps:], sems.at[4]),
    ]
    for load in loads:
        load.start()
    shifted = pltpu.roll(jnp.broadcast_to(small_ref[:, : 2 * taps], (taps, 2 * taps)), 0, 1, stride=1, stride_axis=0)
    toeplitz = halves(shifted)
    high_ref[...], low_ref[...] = toeplitz

    code = small_ref[:, 2 * taps : 2 * taps + rows].astype(jnp.int32)
    owner, sub = code // BIN_DEV, code % BIN_DEV
    owners = NY * NU * NW * NC
    named = lax.broadcasted_iota(jnp.int32, (owners, rows), 0) == owner
    named = jnp.where(named, 1.0, 0.0)
    earlier = lax.broadcasted_iota(jnp.int32, (rows, rows), 0) < lax.broadcasted_iota(jnp.int32, (rows, rows), 1)
    earlier = jnp.where(earlier, 1.0, 0.0).astype(jnp.bfloat16)
    rank = jnp.sum(named * dot(named.astype(jnp.bfloat16), earlier), axis=0, keepdims=True).astype(jnp.int32)
    core, w = owner % NC, owner // NC % NW
    u, y = owner // (NC * NW) % NU, owner // (NC * NW * NU)
    peer = (y * NW + w) * NC + core
    within = u * CAP + rank
    slot = peer * SLOTS + within
    slot_ref[...] = slot
    to_peer = lax.broadcasted_iota(jnp.int32, (PEERS, rows), 0) == peer
    to_peer = jnp.where(to_peer, (sub + 1).astype(jnp.float32), 0.0).astype(jnp.bfloat16)
    column = lax.broadcasted_iota(jnp.int32, (LANES, rows), 0)
    shelf = lax.rem(lax.axis_index(NEAR), SHELVES) * SLOTS
    in_column = jnp.where(column == within + shelf, 1.0, 0.0).astype(jnp.bfloat16)
    label_ref[...] = lax.dot_general(
        to_peer, in_column, (((1,), (1,)), ((), ())), preferred_element_type=jnp.float32
    )

    loads[0].wait()
    loads[1].wait()
    stacked = jnp.concatenate([traces_ref[:, b * taps : (b + 1) * taps] for b in range(count)], axis=0)
    spread = dot_split(halves(stacked), toeplitz)
    pieces = [
        spread[b * rows : (b + 1) * rows, :taps] + spread[(b - 1) * rows : b * rows, taps:] for b in range(1, count)
    ]
    edge_ref[:, :taps] = spread[:rows, :taps]
    edge_ref[:, taps : 2 * taps] = pieces[0]
    edge_ref[:, 2 * taps : 3 * taps] = pieces[-1]
    edge_ref[:, 3 * taps :] = spread[(count - 1) * rows :, taps:]
    loads[2].wait()
    quarters = [map_ref[:, c * LANES : (c + 1) * LANES] for c in range(half // LANES)]
    placed = place_slots(slot, move_out(jnp.concatenate(pieces, axis=1), quarters))
    for c, placed_ref in enumerate(placed_refs):
        placed_ref[...] = placed[:, c * LANES : (c + 1) * LANES]
    loads[3].wait()
    loads[4].wait()


def outer_kernel(before_ref, after_ref, high_ref, low_ref, edge_ref, edge_map_ref, slot_ref, label_ref, *rest):
    *placed_refs, out_ref = rest
    taps = before_ref.shape[1]
    parts = taps // LANES
    length = out_ref.shape[0] // PEERS
    slot = slot_ref[...]

    def put(c, placed):
        for peer in range(PEERS):
            start = peer * length + c * SLOTS
            out_ref[start : start + SLOTS, :] = placed[peer * SLOTS : (peer + 1) * SLOTS, :]

    def put_edge(c, k, window):
        quarters = [edge_map_ref[:, (k + i) * LANES : (k + i + 1) * LANES] for i in range(parts)]
        placed = place_slots(slot, move_out(window, quarters))
        for i in range(parts):
            put(c + i, placed[:, i * LANES : (i + 1) * LANES])

    place = lax.axis_index("section")
    early = dot_split(halves(before_ref[...]), (high_ref[:, taps:], low_ref[:, taps:])) + edge_ref[:, :taps]
    put_edge(0, 0, jnp.concatenate([early, edge_ref[:, taps : 2 * taps]], axis=1))
    late = dot_split(halves(after_ref[...]), (high_ref[:, :taps], low_ref[:, :taps])) + edge_ref[:, 3 * taps :]
    late = jnp.where(place == lax.axis_size("section") - 1, 0.0, late)
    put_edge(parts + len(placed_refs), parts, jnp.concatenate([edge_ref[:, 2 * taps : 3 * taps], late], axis=1))
    for c, placed_ref in enumerate(placed_refs):
        put(parts + c, placed_ref)
    for peer in range(PEERS):
        out_ref[(peer + 1) * length - 1 : (peer + 1) * length, :] = label_ref[peer : peer + 1, :]


def combine_kernel(arrived_ref, out_ref):
    length = arrived_ref.shape[0] // PEERS
    out_length = out_ref.shape[0] // NU
    parts = length // SLOTS
    shelves = []
    for first in range(0, PEERS, SHELVES):
        row = sum(arrived_ref[(peer + 1) * length - 1 : (peer + 1) * length, :] for peer in range(first, first + SHELVES))
        shelves.append(row)
    labels = jnp.concatenate(shelves, axis=1)
    slots = PEERS * SLOTS
    shape = (NU * BIN_DEV, slots)
    row = lax.broadcasted_iota(jnp.int32, shape, 0)
    column = lax.broadcasted_iota(jnp.int32, shape, 1)
    bin_label = (row % BIN_DEV + 1).astype(jnp.float32)
    hit = (labels == bin_label) & (row // BIN_DEV == column % SLOTS // CAP)
    member = jnp.where(hit, 1.0, 0.0).astype(jnp.bfloat16)
    for c in range(0, parts, 2):
        pair = []
        for k in (c, c + 1):
            starts = [peer * length + k * SLOTS for peer in range(PEERS)]
            pair.append(jnp.concatenate([arrived_ref[start : start + SLOTS, :] for start in starts], axis=0))
        total = dot_exact(member, jnp.concatenate(pair, axis=1))
        for k in (0, 1):
            for u in range(NU):
                start = u * out_length + (c + k) * BIN_DEV
                out_ref[start : start + BIN_DEV, :] = total[
                    u * BIN_DEV : (u + 1) * BIN_DEV, k * LANES : (k + 1) * LANES
                ]
    column = lax.broadcasted_iota(jnp.int32, (NU, slots), 1)
    of_owner = (lax.broadcasted_iota(jnp.int32, (NU, slots), 0) == column % SLOTS // CAP) & (labels > 0.0)
    of_owner = jnp.where(of_owner, 1.0, 0.0).astype(jnp.bfloat16)
    of_bin = labels == (lax.broadcasted_iota(jnp.int32, (LANES, slots), 0) + 1).astype(jnp.float32)
    of_bin = jnp.where(of_bin, 1.0, 0.0).astype(jnp.bfloat16)
    fold = lax.dot_general(of_owner, of_bin, (((1,), (1,)), ((), ())), preferred_element_type=jnp.float32)
    for u in range(NU):
        out_ref[(u + 1) * out_length - 1 : (u + 1) * out_length, :] = fold[u : u + 1, :]


def finish_kernel(arrived_ref, out_ref):
    length = arrived_ref.shape[0] // NU
    fold = sum(arrived_ref[(u + 1) * length - 1 : (u + 1) * length, :] for u in range(NU))
    diagonal = lax.broadcasted_iota(jnp.int32, (BIN_DEV, LANES), 0) == lax.broadcasted_iota(jnp.int32, (BIN_DEV, LANES), 1)
    counts = jnp.sum(jnp.where(diagonal, fold, 0.0), axis=1, keepdims=True)
    scale = jnp.sqrt(jnp.maximum(counts, 1.0))
    for c in range(length // BIN_DEV):
        starts = [u * length + c * BIN_DEV for u in range(NU)]
        total = sum(arrived_ref[start : start + BIN_DEV, :] for start in starts)
        out_ref[:, c * LANES : (c + 1) * LANES] = total / scale


VMEM = pl.BlockSpec(memory_space=pltpu.VMEM)
ANY = pl.BlockSpec(memory_space=pl.ANY)
LIMIT = 24 * 1024 * 1024
INNER_LIMIT = 53760


def f32(*shape):
    return jax.ShapeDtypeStruct(shape, jnp.float32)


def correct_inner(small, traces, sample_map):
    rows, width = traces.shape
    taps = (small.shape[1] - LANES) // 2
    inner = (width - 2 * taps) // LANES
    return pl.pallas_call(
        inner_kernel,
        out_shape=(
            jax.ShapeDtypeStruct((taps, 2 * taps), jnp.bfloat16),
            jax.ShapeDtypeStruct((taps, 2 * taps), jnp.bfloat16),
            f32(rows, 4 * taps),
            jax.ShapeDtypeStruct((rows, 2 * taps), jnp.int32),
            jax.ShapeDtypeStruct((1, rows), jnp.int32),
            f32(PEERS, LANES),
        )
        + (f32(PEERS * SLOTS, LANES),) * inner,
        in_specs=[VMEM, ANY, ANY],
        out_specs=(VMEM,) * (6 + inner),
        scratch_shapes=[
            pltpu.VMEM((rows, width), jnp.float32),
            pltpu.VMEM((rows, inner * LANES), jnp.int32),
            pltpu.SemaphoreType.DMA((5,)),
        ],
        name="correct_inner",
        cost_estimate=pl.CostEstimate(flops=500_000_000, bytes_accessed=2_000_000, transcendentals=0),
        compiler_params=pltpu.CompilerParams(vmem_limit_bytes=INNER_LIMIT * 1024),
    )(small, traces, sample_map)


def on_vmem(kernel, shape, name, *operands):
    return pl.pallas_call(
        kernel,
        out_shape=f32(*shape),
        in_specs=[VMEM] * len(operands),
        out_specs=VMEM,
        name=name,
        compiler_params=pltpu.CompilerParams(vmem_limit_bytes=LIMIT),
    )(*operands)


def passed_along(value, axis, steps):
    count = lax.axis_size(axis)
    leading, last = (max(0, -steps), min(count, count - steps))
    return lax.ppermute(value, axis, [(source, source + steps) for source in range(leading, last)])


def exchanged(rows, axes):
    count, lanes = rows.shape
    sent = rows.reshape(count, 1, lanes)
    return lax.all_to_all(sent, axes, split_axis=0, concat_axis=0, tiled=True).reshape(count, lanes)


def per_device(traces, filters, owners, sub_bins, sample_map):
    rows, width = traces.shape
    taps = filters.shape[1]
    before = passed_along(traces[:, width - taps :], "section", 1)
    after = passed_along(traces[:, :taps], "section", -1)
    code = (owners.reshape(1, rows) * BIN_DEV + sub_bins.reshape(1, rows)).astype(jnp.float32)
    small = jnp.pad(filters, ((0, 0), (0, taps + LANES))) + jnp.pad(code, ((0, 0), (2 * taps, LANES - rows)))
    kept = correct_inner(small, traces, sample_map)
    parts = width // LANES
    sent = on_vmem(outer_kernel, (PEERS * (parts * SLOTS + 1), LANES), "correct_outer", before, after, *kept)
    near = exchanged(sent, NEAR)
    summed = on_vmem(combine_kernel, (NU * (parts * BIN_DEV + 1), LANES), "combine", near)
    arrived = exchanged(summed, "u")
    return on_vmem(finish_kernel, (BIN_DEV, width), "finish", arrived)


def solution(mesh):
    fine = Mesh(mesh.devices.reshape(mesh.devices.shape[0], NY, NU, NW, NC), ("section",) + BINS)
    in_specs = (
        P(BINS, "section"),
        P(BINS, None),
        P(BINS, None),
        P(BINS),
        P(BINS, "section"),
    )
    return jax.shard_map(
        per_device, mesh=fine, in_specs=in_specs, out_specs=P(BINS, "section"), check_vma=False
    )
```

```python
import jax
import jax.numpy as jnp
from jax import lax
from jax.experimental import pallas as pl
from jax.experimental.pallas import tpu as pltpu
from jax.sharding import Mesh
from jax.sharding import PartitionSpec as P

BIN_DEV = 8
CAP = 2
LANES = 128
NY, NU, NW, NC = 4, 8, 2, 2
BINS = ("y", "u", "w", "c")
NEAR = ("y", "w", "c")
PEERS = NY * NW * NC
SLOTS = NU * CAP
SHELVES = LANES // SLOTS


def halves(value):
    high = value.astype(jnp.bfloat16)
    low = (value - high.astype(jnp.float32)).astype(jnp.bfloat16)
    return high, low


def dot(a, b):
    return jnp.dot(a, b, preferred_element_type=jnp.float32)


def dot_split(a, b):
    return dot(jnp.concatenate([a[0], a[1], a[0]], axis=1), jnp.concatenate([b[0], b[0], b[1]], axis=0))


def dot_exact(member, value):
    return dot(jnp.concatenate([member, member], axis=1), jnp.concatenate(halves(value), axis=0))


def move_out(window, quarters):
    rows, span = window.shape
    step = pltpu.roll(window, span - 1, 1) - window
    lane = lax.broadcasted_iota(jnp.int32, (rows, LANES), 1)
    moved = []
    for c, quarter in enumerate(quarters):
        place = lane + (quarter >> 2)
        weight = (quarter & 3).astype(jnp.float32) * 0.25
        inside = place & (LANES - 1)
        block = place >> 7
        near = slope = None
        for k in range(3):
            columns = slice((c + k) * LANES, (c + k + 1) * LANES)
            value = jnp.take_along_axis(window[:, columns], inside, axis=1, mode="promise_in_bounds")
            change = jnp.take_along_axis(step[:, columns], inside, axis=1, mode="promise_in_bounds")
            near = value if k == 0 else jnp.where(block == k, value, near)
            slope = change if k == 0 else jnp.where(block == k, change, slope)
        moved.append(near + weight * slope)
    return jnp.concatenate(moved, axis=1)


def place_slots(slot, moved):
    number = lax.broadcasted_iota(jnp.int32, (PEERS * SLOTS, moved.shape[0]), 0)
    member = jnp.where(number == slot, 1.0, 0.0).astype(jnp.bfloat16)
    return dot_exact(member, moved)


def inner_kernel(
    small_ref, traces_hbm, map_hbm,
    high_ref, low_ref, edge_ref, edge_map_ref, slot_ref, label_ref, *rest,
):
    *placed_refs, traces_ref, map_ref, sems = rest
    rows, width = traces_ref.shape
    taps = (small_ref.shape[1] - LANES) // 2
    half = width // 2
    count = width // taps
    loads = []
    for part in range(2):
        columns = pl.ds(part * half, half)
        loads.append(pltpu.make_async_copy(traces_hbm.at[:, columns], traces_ref.at[:, columns], sems.at[part]))
    loads += [
        pltpu.make_async_copy(map_hbm.at[:, taps : taps + half], map_ref, sems.at[2]),
        pltpu.make_async_copy(map_hbm.at[:, :taps], edge_map_ref.at[:, :taps], sems.at[3]),
        pltpu.make_async_copy(map_hbm.at[:, taps + half :], edge_map_ref.at[:, taps:], sems.at[4]),
    ]
    for load in loads:
        load.start()
    shifted = pltpu.roll(jnp.broadcast_to(small_ref[:, : 2 * taps], (taps, 2 * taps)), 0, 1, stride=1, stride_axis=0)
    toeplitz = halves(shifted)
    high_ref[...], low_ref[...] = toeplitz

    code = small_ref[:, 2 * taps : 2 * taps + rows].astype(jnp.int32)
    owner, sub = code // BIN_DEV, code % BIN_DEV
    owners = NY * NU * NW * NC
    named = lax.broadcasted_iota(jnp.int32, (owners, rows), 0) == owner
    named = jnp.where(named, 1.0, 0.0)
    earlier = lax.broadcasted_iota(jnp.int32, (rows, rows), 0) < lax.broadcasted_iota(jnp.int32, (rows, rows), 1)
    earlier = jnp.where(earlier, 1.0, 0.0).astype(jnp.bfloat16)
    rank = jnp.sum(named * dot(named.astype(jnp.bfloat16), earlier), axis=0, keepdims=True).astype(jnp.int32)
    core, w = owner % NC, owner // NC % NW
    u, y = owner // (NC * NW) % NU, owner // (NC * NW * NU)
    peer = (y * NW + w) * NC + core
    within = u * CAP + rank
    slot = peer * SLOTS + within
    slot_ref[...] = slot
    to_peer = lax.broadcasted_iota(jnp.int32, (PEERS, rows), 0) == peer
    to_peer = jnp.where(to_peer, (sub + 1).astype(jnp.float32), 0.0).astype(jnp.bfloat16)
    column = lax.broadcasted_iota(jnp.int32, (LANES, rows), 0)
    shelf = lax.rem(lax.axis_index(NEAR), SHELVES) * SLOTS
    in_column = jnp.where(column == within + shelf, 1.0, 0.0).astype(jnp.bfloat16)
    label_ref[...] = lax.dot_general(
        to_peer, in_column, (((1,), (1,)), ((), ())), preferred_element_type=jnp.float32
    )

    loads[0].wait()
    loads[1].wait()
    stacked = jnp.concatenate([traces_ref[:, b * taps : (b + 1) * taps] for b in range(count)], axis=0)
    spread = dot_split(halves(stacked), toeplitz)
    pieces = [
        spread[b * rows : (b + 1) * rows, :taps] + spread[(b - 1) * rows : b * rows, taps:] for b in range(1, count)
    ]
    edge_ref[:, :taps] = spread[:rows, :taps]
    edge_ref[:, taps : 2 * taps] = pieces[0]
    edge_ref[:, 2 * taps : 3 * taps] = pieces[-1]
    edge_ref[:, 3 * taps :] = spread[(count - 1) * rows :, taps:]
    loads[2].wait()
    quarters = [map_ref[:, c * LANES : (c + 1) * LANES] for c in range(half // LANES)]
    placed = place_slots(slot, move_out(jnp.concatenate(pieces, axis=1), quarters))
    for c, placed_ref in enumerate(placed_refs):
        placed_ref[...] = placed[:, c * LANES : (c + 1) * LANES]
    loads[3].wait()
    loads[4].wait()


def outer_kernel(before_ref, after_ref, high_ref, low_ref, edge_ref, edge_map_ref, slot_ref, label_ref, *rest):
    *placed_refs, out_ref = rest
    taps = before_ref.shape[1]
    parts = taps // LANES
    length = out_ref.shape[0] // PEERS
    slot = slot_ref[...]

    def put(c, placed):
        for peer in range(PEERS):
            start = peer * length + c * SLOTS
            out_ref[start : start + SLOTS, :] = placed[peer * SLOTS : (peer + 1) * SLOTS, :]

    def put_edge(c, k, window):
        quarters = [edge_map_ref[:, (k + i) * LANES : (k + i + 1) * LANES] for i in range(parts)]
        placed = place_slots(slot, move_out(window, quarters))
        for i in range(parts):
            put(c + i, placed[:, i * LANES : (i + 1) * LANES])

    place = lax.axis_index("section")
    early = dot_split(halves(before_ref[...]), (high_ref[:, taps:], low_ref[:, taps:])) + edge_ref[:, :taps]
    put_edge(0, 0, jnp.concatenate([early, edge_ref[:, taps : 2 * taps]], axis=1))
    late = dot_split(halves(after_ref[...]), (high_ref[:, :taps], low_ref[:, :taps])) + edge_ref[:, 3 * taps :]
    late = jnp.where(place == lax.axis_size("section") - 1, 0.0, late)
    put_edge(parts + len(placed_refs), parts, jnp.concatenate([edge_ref[:, 2 * taps : 3 * taps], late], axis=1))
    for c, placed_ref in enumerate(placed_refs):
        put(parts + c, placed_ref)
    for peer in range(PEERS):
        out_ref[(peer + 1) * length - 1 : (peer + 1) * length, :] = label_ref[peer : peer + 1, :]


def combine_kernel(arrived_ref, out_ref):
    length = arrived_ref.shape[0] // PEERS
    out_length = out_ref.shape[0] // NU
    parts = length // SLOTS
    shelves = []
    for first in range(0, PEERS, SHELVES):
        row = sum(arrived_ref[(peer + 1) * length - 1 : (peer + 1) * length, :] for peer in range(first, first + SHELVES))
        shelves.append(row)
    labels = jnp.concatenate(shelves, axis=1)
    slots = PEERS * SLOTS
    shape = (NU * BIN_DEV, slots)
    row = lax.broadcasted_iota(jnp.int32, shape, 0)
    column = lax.broadcasted_iota(jnp.int32, shape, 1)
    bin_label = (row % BIN_DEV + 1).astype(jnp.float32)
    hit = (labels == bin_label) & (row // BIN_DEV == column % SLOTS // CAP)
    member = jnp.where(hit, 1.0, 0.0).astype(jnp.bfloat16)
    for c in range(0, parts, 2):
        pair = []
        for k in (c, c + 1):
            starts = [peer * length + k * SLOTS for peer in range(PEERS)]
            pair.append(jnp.concatenate([arrived_ref[start : start + SLOTS, :] for start in starts], axis=0))
        total = dot_exact(member, jnp.concatenate(pair, axis=1))
        for k in (0, 1):
            for u in range(NU):
                start = u * out_length + (c + k) * BIN_DEV
                out_ref[start : start + BIN_DEV, :] = total[
                    u * BIN_DEV : (u + 1) * BIN_DEV, k * LANES : (k + 1) * LANES
                ]
    column = lax.broadcasted_iota(jnp.int32, (NU, slots), 1)
    of_owner = (lax.broadcasted_iota(jnp.int32, (NU, slots), 0) == column % SLOTS // CAP) & (labels > 0.0)
    of_owner = jnp.where(of_owner, 1.0, 0.0).astype(jnp.bfloat16)
    of_bin = labels == (lax.broadcasted_iota(jnp.int32, (LANES, slots), 0) + 1).astype(jnp.float32)
    of_bin = jnp.where(of_bin, 1.0, 0.0).astype(jnp.bfloat16)
    fold = lax.dot_general(of_owner, of_bin, (((1,), (1,)), ((), ())), preferred_element_type=jnp.float32)
    for u in range(NU):
        out_ref[(u + 1) * out_length - 1 : (u + 1) * out_length, :] = fold[u : u + 1, :]


def finish_kernel(arrived_ref, out_ref):
    length = arrived_ref.shape[0] // NU
    fold = sum(arrived_ref[(u + 1) * length - 1 : (u + 1) * length, :] for u in range(NU))
    diagonal = lax.broadcasted_iota(jnp.int32, (BIN_DEV, LANES), 0) == lax.broadcasted_iota(jnp.int32, (BIN_DEV, LANES), 1)
    counts = jnp.sum(jnp.where(diagonal, fold, 0.0), axis=1, keepdims=True)
    scale = jnp.sqrt(jnp.maximum(counts, 1.0))
    for c in range(length // BIN_DEV):
        starts = [u * length + c * BIN_DEV for u in range(NU)]
        total = sum(arrived_ref[start : start + BIN_DEV, :] for start in starts)
        out_ref[:, c * LANES : (c + 1) * LANES] = total / scale


VMEM = pl.BlockSpec(memory_space=pltpu.VMEM)
ANY = pl.BlockSpec(memory_space=pl.ANY)
LIMIT = 24 * 1024 * 1024
INNER_LIMIT = 53760


def f32(*shape):
    return jax.ShapeDtypeStruct(shape, jnp.float32)


def correct_inner(small, traces, sample_map):
    rows, width = traces.shape
    taps = (small.shape[1] - LANES) // 2
    inner = (width - 2 * taps) // LANES
    return pl.pallas_call(
        inner_kernel,
        out_shape=(
            jax.ShapeDtypeStruct((taps, 2 * taps), jnp.bfloat16),
            jax.ShapeDtypeStruct((taps, 2 * taps), jnp.bfloat16),
            f32(rows, 4 * taps),
            jax.ShapeDtypeStruct((rows, 2 * taps), jnp.int32),
            jax.ShapeDtypeStruct((1, rows), jnp.int32),
            f32(PEERS, LANES),
        )
        + (f32(PEERS * SLOTS, LANES),) * inner,
        in_specs=[VMEM, ANY, ANY],
        out_specs=(VMEM,) * (6 + inner),
        scratch_shapes=[
            pltpu.VMEM((rows, width), jnp.float32),
            pltpu.VMEM((rows, inner * LANES), jnp.int32),
            pltpu.SemaphoreType.DMA((5,)),
        ],
        name="correct_inner",
        cost_estimate=pl.CostEstimate(flops=500_000_000, bytes_accessed=2_000_000, transcendentals=0),
        compiler_params=pltpu.CompilerParams(vmem_limit_bytes=INNER_LIMIT * 1024),
    )(small, traces, sample_map)


def on_vmem(kernel, shape, name, *operands):
    return pl.pallas_call(
        kernel,
        out_shape=f32(*shape),
        in_specs=[VMEM] * len(operands),
        out_specs=VMEM,
        name=name,
        compiler_params=pltpu.CompilerParams(vmem_limit_bytes=LIMIT),
    )(*operands)


def passed_along(value, axis, steps):
    count = lax.axis_size(axis)
    leading, last = (max(0, -steps), min(count, count - steps))
    return lax.ppermute(value, axis, [(source, source + steps) for source in range(leading, last)])


def exchanged(rows, axes):
    count, lanes = rows.shape
    sent = rows.reshape(count, 1, lanes)
    return lax.all_to_all(sent, axes, split_axis=0, concat_axis=0, tiled=True).reshape(count, lanes)


def per_device(traces, filters, owners, sub_bins, sample_map):
    rows, width = traces.shape
    taps = filters.shape[1]
    before = passed_along(traces[:, width - taps :], "section", 1)
    after = passed_along(traces[:, :taps], "section", -1)
    around = ((0, 0), (2 * taps, LANES - rows))
    owner, sub = jnp.pad(owners.reshape(1, rows), around), jnp.pad(sub_bins.reshape(1, rows), around)
    small = jnp.pad(filters, ((0, 0), (0, taps + LANES))) + (owner * BIN_DEV + sub).astype(jnp.float32)
    kept = correct_inner(small, traces, sample_map)
    parts = width // LANES
    sent = on_vmem(outer_kernel, (PEERS * (parts * SLOTS + 1), LANES), "correct_outer", before, after, *kept)
    near = exchanged(sent, NEAR)
    summed = on_vmem(combine_kernel, (NU * (parts * BIN_DEV + 1), LANES), "combine", near)
    arrived = exchanged(summed, "u")
    return on_vmem(finish_kernel, (BIN_DEV, width), "finish", arrived)


def solution(mesh):
    fine = Mesh(mesh.devices.reshape(mesh.devices.shape[0], NY, NU, NW, NC), ("section",) + BINS)
    in_specs = (
        P(BINS, "section"),
        P(BINS, None),
        P(BINS, None),
        P(BINS),
        P(BINS, "section"),
    )
    return jax.shard_map(
        per_device, mesh=fine, in_specs=in_specs, out_specs=P(BINS, "section"), check_vma=False
    )
```

```python
import jax
import jax.numpy as jnp
from jax import lax
from jax.experimental import pallas as pl
from jax.experimental.pallas import tpu as pltpu
from jax.sharding import Mesh
from jax.sharding import PartitionSpec as P

BIN_DEV = 8
CAP = 2
LANES = 128
NY, NU, NW, NC = 4, 8, 2, 2
BINS = ("y", "u", "w", "c")
NEAR = ("y", "w", "c")
PEERS = NY * NW * NC
SLOTS = NU * CAP
SHELVES = LANES // SLOTS


def halves(value):
    high = value.astype(jnp.bfloat16)
    low = (value - high.astype(jnp.float32)).astype(jnp.bfloat16)
    return high, low


def dot(a, b):
    return jnp.dot(a, b, preferred_element_type=jnp.float32)


def dot_split(a, b):
    return dot(jnp.concatenate([a[0], a[1], a[0]], axis=1), jnp.concatenate([b[0], b[0], b[1]], axis=0))


def dot_exact(member, value):
    return dot(jnp.concatenate([member, member], axis=1), jnp.concatenate(halves(value), axis=0))


def move_out(window, quarters):
    rows, span = window.shape
    step = pltpu.roll(window, span - 1, 1) - window
    lane = lax.broadcasted_iota(jnp.int32, (rows, LANES), 1)
    moved = []
    for c, quarter in enumerate(quarters):
        place = lane + (quarter >> 2)
        weight = (quarter & 3).astype(jnp.float32) * 0.25
        inside = place & (LANES - 1)
        block = place >> 7
        near = slope = None
        for k in range(3):
            columns = slice((c + k) * LANES, (c + k + 1) * LANES)
            value = jnp.take_along_axis(window[:, columns], inside, axis=1, mode="promise_in_bounds")
            change = jnp.take_along_axis(step[:, columns], inside, axis=1, mode="promise_in_bounds")
            near = value if k == 0 else jnp.where(block == k, value, near)
            slope = change if k == 0 else jnp.where(block == k, change, slope)
        moved.append(near + weight * slope)
    return jnp.concatenate(moved, axis=1)


def place_slots(slot, moved):
    number = lax.broadcasted_iota(jnp.int32, (PEERS * SLOTS, moved.shape[0]), 0)
    member = jnp.where(number == slot, 1.0, 0.0).astype(jnp.bfloat16)
    return dot_exact(member, moved)


def inner_kernel(
    small_ref, traces_hbm, map_hbm,
    high_ref, low_ref, edge_ref, edge_map_ref, slot_ref, label_ref, *rest,
):
    *placed_refs, traces_ref, map_ref, sems = rest
    rows, width = traces_ref.shape
    taps = (small_ref.shape[1] - LANES) // 2
    half = width // 2
    count = width // taps
    loads = []
    for part in range(2):
        columns = pl.ds(part * half, half)
        loads.append(pltpu.make_async_copy(traces_hbm.at[:, columns], traces_ref.at[:, columns], sems.at[part]))
    loads += [
        pltpu.make_async_copy(map_hbm.at[:, taps : taps + half], map_ref, sems.at[2]),
        pltpu.make_async_copy(map_hbm.at[:, :taps], edge_map_ref.at[:, :taps], sems.at[3]),
        pltpu.make_async_copy(map_hbm.at[:, taps + half :], edge_map_ref.at[:, taps:], sems.at[4]),
    ]
    for load in loads:
        load.start()
    shifted = pltpu.roll(jnp.broadcast_to(small_ref[:, : 2 * taps], (taps, 2 * taps)), 0, 1, stride=1, stride_axis=0)
    toeplitz = halves(shifted)
    high_ref[...], low_ref[...] = toeplitz

    code = small_ref[:, 2 * taps : 2 * taps + rows].astype(jnp.int32)
    owner, sub = code // BIN_DEV, code % BIN_DEV
    owners = NY * NU * NW * NC
    named = lax.broadcasted_iota(jnp.int32, (owners, rows), 0) == owner
    named = jnp.where(named, 1.0, 0.0)
    earlier = lax.broadcasted_iota(jnp.int32, (rows, rows), 0) < lax.broadcasted_iota(jnp.int32, (rows, rows), 1)
    earlier = jnp.where(earlier, 1.0, 0.0).astype(jnp.bfloat16)
    rank = jnp.sum(named * dot(named.astype(jnp.bfloat16), earlier), axis=0, keepdims=True).astype(jnp.int32)
    core, w = owner % NC, owner // NC % NW
    u, y = owner // (NC * NW) % NU, owner // (NC * NW * NU)
    peer = (y * NW + w) * NC + core
    within = u * CAP + rank
    slot = peer * SLOTS + within
    slot_ref[...] = slot
    to_peer = lax.broadcasted_iota(jnp.int32, (PEERS, rows), 0) == peer
    to_peer = jnp.where(to_peer, (sub + 1).astype(jnp.float32), 0.0).astype(jnp.bfloat16)
    column = lax.broadcasted_iota(jnp.int32, (LANES, rows), 0)
    shelf = lax.rem(lax.axis_index(NEAR), SHELVES) * SLOTS
    in_column = jnp.where(column == within + shelf, 1.0, 0.0).astype(jnp.bfloat16)
    label_ref[...] = lax.dot_general(
        to_peer, in_column, (((1,), (1,)), ((), ())), preferred_element_type=jnp.float32
    )

    loads[0].wait()
    loads[1].wait()
    stacked = jnp.concatenate([traces_ref[:, b * taps : (b + 1) * taps] for b in range(count)], axis=0)
    spread = dot_split(halves(stacked), toeplitz)
    pieces = [
        spread[b * rows : (b + 1) * rows, :taps] + spread[(b - 1) * rows : b * rows, taps:] for b in range(1, count)
    ]
    edge_ref[:, :taps] = spread[:rows, :taps]
    edge_ref[:, taps : 2 * taps] = pieces[0]
    edge_ref[:, 2 * taps : 3 * taps] = pieces[-1]
    edge_ref[:, 3 * taps :] = spread[(count - 1) * rows :, taps:]
    loads[2].wait()
    quarters = [map_ref[:, c * LANES : (c + 1) * LANES] for c in range(half // LANES)]
    placed = place_slots(slot, move_out(jnp.concatenate(pieces, axis=1), quarters))
    for c, placed_ref in enumerate(placed_refs):
        placed_ref[...] = placed[:, c * LANES : (c + 1) * LANES]
    loads[3].wait()
    loads[4].wait()


def outer_kernel(before_ref, after_ref, high_ref, low_ref, edge_ref, edge_map_ref, slot_ref, label_ref, *rest):
    *placed_refs, out_ref = rest
    taps = before_ref.shape[1]
    parts = taps // LANES
    length = out_ref.shape[0] // PEERS
    slot = slot_ref[...]

    def put(c, placed):
        for peer in range(PEERS):
            start = peer * length + c * SLOTS
            out_ref[start : start + SLOTS, :] = placed[peer * SLOTS : (peer + 1) * SLOTS, :]

    def moved(k, window):
        return move_out(window, [edge_map_ref[:, (k + i) * LANES : (k + i + 1) * LANES] for i in range(parts)])

    early = dot_split(halves(before_ref[...]), (high_ref[:, taps:], low_ref[:, taps:])) + edge_ref[:, :taps]
    late = dot_split(halves(after_ref[...]), (high_ref[:, :taps], low_ref[:, :taps])) + edge_ref[:, 3 * taps :]
    late = jnp.where(lax.axis_index("section") == lax.axis_size("section") - 1, 0.0, late)
    first = moved(0, jnp.concatenate([early, edge_ref[:, taps : 2 * taps]], axis=1))
    last = moved(parts, jnp.concatenate([edge_ref[:, 2 * taps : 3 * taps], late], axis=1))
    placed = place_slots(slot, jnp.concatenate([first, last], axis=1))
    places = [*range(parts), *range(parts + len(placed_refs), 2 * parts + len(placed_refs))]
    for i, c in enumerate(places):
        put(c, placed[:, i * LANES : (i + 1) * LANES])
    for c, placed_ref in enumerate(placed_refs):
        put(parts + c, placed_ref)
    for peer in range(PEERS):
        out_ref[(peer + 1) * length - 1 : (peer + 1) * length, :] = label_ref[peer : peer + 1, :]


def combine_kernel(arrived_ref, out_ref):
    length = arrived_ref.shape[0] // PEERS
    out_length = out_ref.shape[0] // NU
    parts = length // SLOTS
    shelves = []
    for first in range(0, PEERS, SHELVES):
        row = sum(arrived_ref[(peer + 1) * length - 1 : (peer + 1) * length, :] for peer in range(first, first + SHELVES))
        shelves.append(row)
    labels = jnp.concatenate(shelves, axis=1)
    slots = PEERS * SLOTS
    shape = (NU * BIN_DEV, slots)
    row = lax.broadcasted_iota(jnp.int32, shape, 0)
    column = lax.broadcasted_iota(jnp.int32, shape, 1)
    bin_label = (row % BIN_DEV + 1).astype(jnp.float32)
    hit = (labels == bin_label) & (row // BIN_DEV == column % SLOTS // CAP)
    member = jnp.where(hit, 1.0, 0.0).astype(jnp.bfloat16)
    for c in range(0, parts, 2):
        pair = []
        for k in (c, c + 1):
            starts = [peer * length + k * SLOTS for peer in range(PEERS)]
            pair.append(jnp.concatenate([arrived_ref[start : start + SLOTS, :] for start in starts], axis=0))
        total = dot_exact(member, jnp.concatenate(pair, axis=1))
        for k in (0, 1):
            for u in range(NU):
                start = u * out_length + (c + k) * BIN_DEV
                out_ref[start : start + BIN_DEV, :] = total[
                    u * BIN_DEV : (u + 1) * BIN_DEV, k * LANES : (k + 1) * LANES
                ]
    column = lax.broadcasted_iota(jnp.int32, (NU, slots), 1)
    of_owner = (lax.broadcasted_iota(jnp.int32, (NU, slots), 0) == column % SLOTS // CAP) & (labels > 0.0)
    of_owner = jnp.where(of_owner, 1.0, 0.0).astype(jnp.bfloat16)
    of_bin = labels == (lax.broadcasted_iota(jnp.int32, (LANES, slots), 0) + 1).astype(jnp.float32)
    of_bin = jnp.where(of_bin, 1.0, 0.0).astype(jnp.bfloat16)
    fold = lax.dot_general(of_owner, of_bin, (((1,), (1,)), ((), ())), preferred_element_type=jnp.float32)
    for u in range(NU):
        out_ref[(u + 1) * out_length - 1 : (u + 1) * out_length, :] = fold[u : u + 1, :]


def finish_kernel(arrived_ref, out_ref):
    length = arrived_ref.shape[0] // NU
    fold = sum(arrived_ref[(u + 1) * length - 1 : (u + 1) * length, :] for u in range(NU))
    diagonal = lax.broadcasted_iota(jnp.int32, (BIN_DEV, LANES), 0) == lax.broadcasted_iota(jnp.int32, (BIN_DEV, LANES), 1)
    counts = jnp.sum(jnp.where(diagonal, fold, 0.0), axis=1, keepdims=True)
    scale = jnp.sqrt(jnp.maximum(counts, 1.0))
    for c in range(length // BIN_DEV):
        starts = [u * length + c * BIN_DEV for u in range(NU)]
        total = sum(arrived_ref[start : start + BIN_DEV, :] for start in starts)
        out_ref[:, c * LANES : (c + 1) * LANES] = total / scale


VMEM = pl.BlockSpec(memory_space=pltpu.VMEM)
ANY = pl.BlockSpec(memory_space=pl.ANY)
LIMIT = 24 * 1024 * 1024
INNER_LIMIT = 53760


def f32(*shape):
    return jax.ShapeDtypeStruct(shape, jnp.float32)


def correct_inner(small, traces, sample_map):
    rows, width = traces.shape
    taps = (small.shape[1] - LANES) // 2
    inner = (width - 2 * taps) // LANES
    return pl.pallas_call(
        inner_kernel,
        out_shape=(
            jax.ShapeDtypeStruct((taps, 2 * taps), jnp.bfloat16),
            jax.ShapeDtypeStruct((taps, 2 * taps), jnp.bfloat16),
            f32(rows, 4 * taps),
            jax.ShapeDtypeStruct((rows, 2 * taps), jnp.int32),
            jax.ShapeDtypeStruct((1, rows), jnp.int32),
            f32(PEERS, LANES),
        )
        + (f32(PEERS * SLOTS, LANES),) * inner,
        in_specs=[VMEM, ANY, ANY],
        out_specs=(VMEM,) * (6 + inner),
        scratch_shapes=[
            pltpu.VMEM((rows, width), jnp.float32),
            pltpu.VMEM((rows, inner * LANES), jnp.int32),
            pltpu.SemaphoreType.DMA((5,)),
        ],
        name="correct_inner",
        cost_estimate=pl.CostEstimate(flops=500_000_000, bytes_accessed=2_000_000, transcendentals=0),
        compiler_params=pltpu.CompilerParams(vmem_limit_bytes=INNER_LIMIT * 1024),
    )(small, traces, sample_map)


def on_vmem(kernel, shape, name, *operands):
    return pl.pallas_call(
        kernel,
        out_shape=f32(*shape),
        in_specs=[VMEM] * len(operands),
        out_specs=VMEM,
        name=name,
        compiler_params=pltpu.CompilerParams(vmem_limit_bytes=LIMIT),
    )(*operands)


def passed_along(value, axis, steps):
    count = lax.axis_size(axis)
    leading, last = (max(0, -steps), min(count, count - steps))
    return lax.ppermute(value, axis, [(source, source + steps) for source in range(leading, last)])


def exchanged(rows, axes):
    count, lanes = rows.shape
    sent = rows.reshape(count, 1, lanes)
    return lax.all_to_all(sent, axes, split_axis=0, concat_axis=0, tiled=True).reshape(count, lanes)


def per_device(traces, filters, owners, sub_bins, sample_map):
    rows, width = traces.shape
    taps = filters.shape[1]
    before = passed_along(traces[:, width - taps :], "section", 1)
    after = passed_along(traces[:, :taps], "section", -1)
    around = ((0, 0), (2 * taps, LANES - rows))
    owner, sub = jnp.pad(owners.reshape(1, rows), around), jnp.pad(sub_bins.reshape(1, rows), around)
    small = jnp.pad(filters, ((0, 0), (0, taps + LANES))) + (owner * BIN_DEV + sub).astype(jnp.float32)
    kept = correct_inner(small, traces, sample_map)
    parts = width // LANES
    sent = on_vmem(outer_kernel, (PEERS * (parts * SLOTS + 1), LANES), "correct_outer", before, after, *kept)
    near = exchanged(sent, NEAR)
    summed = on_vmem(combine_kernel, (NU * (parts * BIN_DEV + 1), LANES), "combine", near)
    arrived = exchanged(summed, "u")
    return on_vmem(finish_kernel, (BIN_DEV, width), "finish", arrived)


def solution(mesh):
    fine = Mesh(mesh.devices.reshape(mesh.devices.shape[0], NY, NU, NW, NC), ("section",) + BINS)
    in_specs = (
        P(BINS, "section"),
        P(BINS, None),
        P(BINS, None),
        P(BINS),
        P(BINS, "section"),
    )
    return jax.shard_map(
        per_device, mesh=fine, in_specs=in_specs, out_specs=P(BINS, "section"), check_vma=False
    )
```

```python
import jax
import jax.numpy as jnp
from jax import lax
from jax.experimental import pallas as pl
from jax.experimental.pallas import tpu as pltpu
from jax.sharding import Mesh
from jax.sharding import PartitionSpec as P

BIN_DEV = 8
CAP = 2
LANES = 128
NY, NU, NW, NC = 4, 8, 2, 2
BINS = ("y", "u", "w", "c")
NEAR = ("y", "w", "c")
PEERS = NY * NW * NC
SLOTS = NU * CAP
SHELVES = LANES // SLOTS


def halves(value):
    high = value.astype(jnp.bfloat16)
    low = (value - high.astype(jnp.float32)).astype(jnp.bfloat16)
    return high, low


def dot(a, b):
    return jnp.dot(a, b, preferred_element_type=jnp.float32)


def dot_split(a, b):
    return dot(jnp.concatenate([a[0], a[1], a[0]], axis=1), jnp.concatenate([b[0], b[0], b[1]], axis=0))


def dot_exact(member, value):
    return dot(jnp.concatenate([member, member], axis=1), jnp.concatenate(halves(value), axis=0))


def move_out(window, quarters):
    rows, span = window.shape
    step = pltpu.roll(window, span - 1, 1) - window
    lane = lax.broadcasted_iota(jnp.int32, (rows, LANES), 1)
    moved = []
    for c, quarter in enumerate(quarters):
        place = lane + (quarter >> 2)
        weight = (quarter & 3).astype(jnp.float32) * 0.25
        inside = place & (LANES - 1)
        block = place >> 7
        near = slope = None
        for k in range(3):
            columns = slice((c + k) * LANES, (c + k + 1) * LANES)
            value = jnp.take_along_axis(window[:, columns], inside, axis=1, mode="promise_in_bounds")
            change = jnp.take_along_axis(step[:, columns], inside, axis=1, mode="promise_in_bounds")
            near = value if k == 0 else jnp.where(block == k, value, near)
            slope = change if k == 0 else jnp.where(block == k, change, slope)
        moved.append(near + weight * slope)
    return jnp.concatenate(moved, axis=1)


def place_slots(slot, moved):
    number = lax.broadcasted_iota(jnp.int32, (PEERS * SLOTS, moved.shape[0]), 0)
    member = jnp.where(number == slot, 1.0, 0.0).astype(jnp.bfloat16)
    return dot_exact(member, moved)


def inner_kernel(
    small_ref, traces_hbm, map_hbm,
    high_ref, low_ref, edge_ref, edge_map_ref, slot_ref, label_ref, *rest,
):
    *placed_refs, traces_ref, map_ref, sems = rest
    rows, width = traces_ref.shape
    taps = (small_ref.shape[1] - LANES) // 2
    half = width // 2
    count = width // taps
    loads = []
    for part in range(2):
        some = pl.ds(part * (rows // 2), rows // 2)
        loads.append(pltpu.make_async_copy(traces_hbm.at[some, :], traces_ref.at[some, :], sems.at[part]))
    loads += [
        pltpu.make_async_copy(map_hbm.at[:, taps : taps + half], map_ref, sems.at[2]),
        pltpu.make_async_copy(map_hbm.at[:, :taps], edge_map_ref.at[:, :taps], sems.at[3]),
        pltpu.make_async_copy(map_hbm.at[:, taps + half :], edge_map_ref.at[:, taps:], sems.at[4]),
    ]
    for load in loads:
        load.start()
    shifted = pltpu.roll(jnp.broadcast_to(small_ref[:, : 2 * taps], (taps, 2 * taps)), 0, 1, stride=1, stride_axis=0)
    toeplitz = halves(shifted)
    high_ref[...], low_ref[...] = toeplitz

    code = small_ref[:, 2 * taps : 2 * taps + rows].astype(jnp.int32)
    owner, sub = code // BIN_DEV, code % BIN_DEV
    owners = NY * NU * NW * NC
    named = lax.broadcasted_iota(jnp.int32, (owners, rows), 0) == owner
    named = jnp.where(named, 1.0, 0.0)
    earlier = lax.broadcasted_iota(jnp.int32, (rows, rows), 0) < lax.broadcasted_iota(jnp.int32, (rows, rows), 1)
    earlier = jnp.where(earlier, 1.0, 0.0).astype(jnp.bfloat16)
    rank = jnp.sum(named * dot(named.astype(jnp.bfloat16), earlier), axis=0, keepdims=True).astype(jnp.int32)
    core, w = owner % NC, owner // NC % NW
    u, y = owner // (NC * NW) % NU, owner // (NC * NW * NU)
    peer = (y * NW + w) * NC + core
    within = u * CAP + rank
    slot = peer * SLOTS + within
    slot_ref[...] = slot
    to_peer = lax.broadcasted_iota(jnp.int32, (PEERS, rows), 0) == peer
    to_peer = jnp.where(to_peer, (sub + 1).astype(jnp.float32), 0.0).astype(jnp.bfloat16)
    column = lax.broadcasted_iota(jnp.int32, (LANES, rows), 0)
    shelf = lax.rem(lax.axis_index(NEAR), SHELVES) * SLOTS
    in_column = jnp.where(column == within + shelf, 1.0, 0.0).astype(jnp.bfloat16)
    label_ref[...] = lax.dot_general(
        to_peer, in_column, (((1,), (1,)), ((), ())), preferred_element_type=jnp.float32
    )

    loads[0].wait()
    loads[1].wait()
    stacked = jnp.concatenate([traces_ref[:, b * taps : (b + 1) * taps] for b in range(count)], axis=0)
    spread = dot_split(halves(stacked), toeplitz)
    pieces = [
        spread[b * rows : (b + 1) * rows, :taps] + spread[(b - 1) * rows : b * rows, taps:] for b in range(1, count)
    ]
    edge_ref[:, :taps] = spread[:rows, :taps]
    edge_ref[:, taps : 2 * taps] = pieces[0]
    edge_ref[:, 2 * taps : 3 * taps] = pieces[-1]
    edge_ref[:, 3 * taps :] = spread[(count - 1) * rows :, taps:]
    loads[2].wait()
    quarters = [map_ref[:, c * LANES : (c + 1) * LANES] for c in range(half // LANES)]
    placed = place_slots(slot, move_out(jnp.concatenate(pieces, axis=1), quarters))
    for c, placed_ref in enumerate(placed_refs):
        placed_ref[...] = placed[:, c * LANES : (c + 1) * LANES]
    loads[3].wait()
    loads[4].wait()


def outer_kernel(before_ref, after_ref, high_ref, low_ref, edge_ref, edge_map_ref, slot_ref, label_ref, *rest):
    *placed_refs, out_ref = rest
    taps = before_ref.shape[1]
    parts = taps // LANES
    length = out_ref.shape[0] // PEERS
    slot = slot_ref[...]

    def put(c, placed):
        for peer in range(PEERS):
            start = peer * length + c * SLOTS
            out_ref[start : start + SLOTS, :] = placed[peer * SLOTS : (peer + 1) * SLOTS, :]

    def moved(k, window):
        return move_out(window, [edge_map_ref[:, (k + i) * LANES : (k + i + 1) * LANES] for i in range(parts)])

    early = dot_split(halves(before_ref[...]), (high_ref[:, taps:], low_ref[:, taps:])) + edge_ref[:, :taps]
    late = dot_split(halves(after_ref[...]), (high_ref[:, :taps], low_ref[:, :taps])) + edge_ref[:, 3 * taps :]
    late = jnp.where(lax.axis_index("section") == lax.axis_size("section") - 1, 0.0, late)
    first = moved(0, jnp.concatenate([early, edge_ref[:, taps : 2 * taps]], axis=1))
    last = moved(parts, jnp.concatenate([edge_ref[:, 2 * taps : 3 * taps], late], axis=1))
    placed = place_slots(slot, jnp.concatenate([first, last], axis=1))
    places = [*range(parts), *range(parts + len(placed_refs), 2 * parts + len(placed_refs))]
    for i, c in enumerate(places):
        put(c, placed[:, i * LANES : (i + 1) * LANES])
    for c, placed_ref in enumerate(placed_refs):
        put(parts + c, placed_ref)
    for peer in range(PEERS):
        out_ref[(peer + 1) * length - 1 : (peer + 1) * length, :] = label_ref[peer : peer + 1, :]


def combine_kernel(arrived_ref, out_ref):
    length = arrived_ref.shape[0] // PEERS
    out_length = out_ref.shape[0] // NU
    parts = length // SLOTS
    shelves = []
    for first in range(0, PEERS, SHELVES):
        row = sum(arrived_ref[(peer + 1) * length - 1 : (peer + 1) * length, :] for peer in range(first, first + SHELVES))
        shelves.append(row)
    labels = jnp.concatenate(shelves, axis=1)
    slots = PEERS * SLOTS
    shape = (NU * BIN_DEV, slots)
    row = lax.broadcasted_iota(jnp.int32, shape, 0)
    column = lax.broadcasted_iota(jnp.int32, shape, 1)
    bin_label = (row % BIN_DEV + 1).astype(jnp.float32)
    hit = (labels == bin_label) & (row // BIN_DEV == column % SLOTS // CAP)
    member = jnp.where(hit, 1.0, 0.0).astype(jnp.bfloat16)
    for c in range(0, parts, 2):
        pair = []
        for k in (c, c + 1):
            starts = [peer * length + k * SLOTS for peer in range(PEERS)]
            pair.append(jnp.concatenate([arrived_ref[start : start + SLOTS, :] for start in starts], axis=0))
        total = dot_exact(member, jnp.concatenate(pair, axis=1))
        for k in (0, 1):
            for u in range(NU):
                start = u * out_length + (c + k) * BIN_DEV
                out_ref[start : start + BIN_DEV, :] = total[
                    u * BIN_DEV : (u + 1) * BIN_DEV, k * LANES : (k + 1) * LANES
                ]
    column = lax.broadcasted_iota(jnp.int32, (NU, slots), 1)
    of_owner = (lax.broadcasted_iota(jnp.int32, (NU, slots), 0) == column % SLOTS // CAP) & (labels > 0.0)
    of_owner = jnp.where(of_owner, 1.0, 0.0).astype(jnp.bfloat16)
    of_bin = labels == (lax.broadcasted_iota(jnp.int32, (LANES, slots), 0) + 1).astype(jnp.float32)
    of_bin = jnp.where(of_bin, 1.0, 0.0).astype(jnp.bfloat16)
    fold = lax.dot_general(of_owner, of_bin, (((1,), (1,)), ((), ())), preferred_element_type=jnp.float32)
    for u in range(NU):
        out_ref[(u + 1) * out_length - 1 : (u + 1) * out_length, :] = fold[u : u + 1, :]


def finish_kernel(arrived_ref, out_ref):
    length = arrived_ref.shape[0] // NU
    fold = sum(arrived_ref[(u + 1) * length - 1 : (u + 1) * length, :] for u in range(NU))
    diagonal = lax.broadcasted_iota(jnp.int32, (BIN_DEV, LANES), 0) == lax.broadcasted_iota(jnp.int32, (BIN_DEV, LANES), 1)
    counts = jnp.sum(jnp.where(diagonal, fold, 0.0), axis=1, keepdims=True)
    scale = jnp.sqrt(jnp.maximum(counts, 1.0))
    for c in range(length // BIN_DEV):
        starts = [u * length + c * BIN_DEV for u in range(NU)]
        total = sum(arrived_ref[start : start + BIN_DEV, :] for start in starts)
        out_ref[:, c * LANES : (c + 1) * LANES] = total / scale


VMEM = pl.BlockSpec(memory_space=pltpu.VMEM)
ANY = pl.BlockSpec(memory_space=pl.ANY)
LIMIT = 24 * 1024 * 1024
INNER_LIMIT = 53760


def f32(*shape):
    return jax.ShapeDtypeStruct(shape, jnp.float32)


def correct_inner(small, traces, sample_map):
    rows, width = traces.shape
    taps = (small.shape[1] - LANES) // 2
    inner = (width - 2 * taps) // LANES
    return pl.pallas_call(
        inner_kernel,
        out_shape=(
            jax.ShapeDtypeStruct((taps, 2 * taps), jnp.bfloat16),
            jax.ShapeDtypeStruct((taps, 2 * taps), jnp.bfloat16),
            f32(rows, 4 * taps),
            jax.ShapeDtypeStruct((rows, 2 * taps), jnp.int32),
            jax.ShapeDtypeStruct((1, rows), jnp.int32),
            f32(PEERS, LANES),
        )
        + (f32(PEERS * SLOTS, LANES),) * inner,
        in_specs=[VMEM, ANY, ANY],
        out_specs=(VMEM,) * (6 + inner),
        scratch_shapes=[
            pltpu.VMEM((rows, width), jnp.float32),
            pltpu.VMEM((rows, inner * LANES), jnp.int32),
            pltpu.SemaphoreType.DMA((5,)),
        ],
        name="correct_inner",
        cost_estimate=pl.CostEstimate(flops=500_000_000, bytes_accessed=2_000_000, transcendentals=0),
        compiler_params=pltpu.CompilerParams(vmem_limit_bytes=INNER_LIMIT * 1024),
    )(small, traces, sample_map)


def on_vmem(kernel, shape, name, *operands):
    return pl.pallas_call(
        kernel,
        out_shape=f32(*shape),
        in_specs=[VMEM] * len(operands),
        out_specs=VMEM,
        name=name,
        compiler_params=pltpu.CompilerParams(vmem_limit_bytes=LIMIT),
    )(*operands)


def passed_along(value, axis, steps):
    count = lax.axis_size(axis)
    leading, last = (max(0, -steps), min(count, count - steps))
    return lax.ppermute(value, axis, [(source, source + steps) for source in range(leading, last)])


def exchanged(rows, axes):
    count, lanes = rows.shape
    sent = rows.reshape(count, 1, lanes)
    return lax.all_to_all(sent, axes, split_axis=0, concat_axis=0, tiled=True).reshape(count, lanes)


def per_device(traces, filters, owners, sub_bins, sample_map):
    rows, width = traces.shape
    taps = filters.shape[1]
    before = passed_along(traces[:, width - taps :], "section", 1)
    after = passed_along(traces[:, :taps], "section", -1)
    around = ((0, 0), (2 * taps, LANES - rows))
    owner, sub = jnp.pad(owners.reshape(1, rows), around), jnp.pad(sub_bins.reshape(1, rows), around)
    small = jnp.pad(filters, ((0, 0), (0, taps + LANES))) + (owner * BIN_DEV + sub).astype(jnp.float32)
    kept = correct_inner(small, traces, sample_map)
    parts = width // LANES
    sent = on_vmem(outer_kernel, (PEERS * (parts * SLOTS + 1), LANES), "correct_outer", before, after, *kept)
    near = exchanged(sent, NEAR)
    summed = on_vmem(combine_kernel, (NU * (parts * BIN_DEV + 1), LANES), "combine", near)
    arrived = exchanged(summed, "u")
    return on_vmem(finish_kernel, (BIN_DEV, width), "finish", arrived)


def solution(mesh):
    fine = Mesh(mesh.devices.reshape(mesh.devices.shape[0], NY, NU, NW, NC), ("section",) + BINS)
    in_specs = (
        P(BINS, "section"),
        P(BINS, None),
        P(BINS, None),
        P(BINS),
        P(BINS, "section"),
    )
    return jax.shard_map(
        per_device, mesh=fine, in_specs=in_specs, out_specs=P(BINS, "section"), check_vma=False
    )
```

```python
import jax
import jax.numpy as jnp
from jax import lax
from jax.experimental import pallas as pl
from jax.experimental.pallas import tpu as pltpu
from jax.sharding import Mesh
from jax.sharding import PartitionSpec as P

BIN_DEV = 8
CAP = 2
LANES = 128
NY, NU, NW, NC = 4, 8, 2, 2
BINS = ("y", "u", "w", "c")
NEAR = ("y", "w", "c")
PEERS = NY * NW * NC
SLOTS = NU * CAP
SHELVES = LANES // SLOTS


def halves(value):
    high = value.astype(jnp.bfloat16)
    low = (value - high.astype(jnp.float32)).astype(jnp.bfloat16)
    return high, low


def dot(a, b):
    return jnp.dot(a, b, preferred_element_type=jnp.float32)


def dot_split(a, b):
    return dot(jnp.concatenate([a[0], a[1], a[0]], axis=1), jnp.concatenate([b[0], b[0], b[1]], axis=0))


def dot_exact(member, value):
    return dot(jnp.concatenate([member, member], axis=1), jnp.concatenate(halves(value), axis=0))


def move_out(window, quarters):
    rows, span = window.shape
    step = pltpu.roll(window, span - 1, 1) - window
    lane = lax.broadcasted_iota(jnp.int32, (rows, LANES), 1)
    moved = []
    for c, quarter in enumerate(quarters):
        place = lane + (quarter >> 2)
        weight = (quarter & 3).astype(jnp.float32) * 0.25
        inside = place & (LANES - 1)
        block = place >> 7
        near = slope = None
        for k in range(3):
            columns = slice((c + k) * LANES, (c + k + 1) * LANES)
            value = jnp.take_along_axis(window[:, columns], inside, axis=1, mode="promise_in_bounds")
            change = jnp.take_along_axis(step[:, columns], inside, axis=1, mode="promise_in_bounds")
            near = value if k == 0 else jnp.where(block == k, value, near)
            slope = change if k == 0 else jnp.where(block == k, change, slope)
        moved.append(near + weight * slope)
    return jnp.concatenate(moved, axis=1)


def place_slots(slot, moved):
    number = lax.broadcasted_iota(jnp.int32, (PEERS * SLOTS, moved.shape[0]), 0)
    member = jnp.where(number == slot, 1.0, 0.0).astype(jnp.bfloat16)
    return dot_exact(member, moved)


def inner_kernel(
    small_ref, traces_hbm, map_hbm,
    high_ref, low_ref, edge_ref, edge_map_ref, slot_ref, label_ref, *rest,
):
    *placed_refs, traces_ref, map_ref, sems = rest
    rows, width = traces_ref.shape
    taps = (small_ref.shape[1] - LANES) // 2
    half = width // 2
    count = width // taps
    loads = []
    for part in range(2):
        some = pl.ds(part * (rows // 2), rows // 2)
        loads.append(pltpu.make_async_copy(traces_hbm.at[some, :], traces_ref.at[some, :], sems.at[part]))
    loads += [
        pltpu.make_async_copy(map_hbm.at[:, taps : taps + half], map_ref, sems.at[2]),
        pltpu.make_async_copy(map_hbm.at[:, :taps], edge_map_ref.at[:, :taps], sems.at[3]),
        pltpu.make_async_copy(map_hbm.at[:, taps + half :], edge_map_ref.at[:, taps:], sems.at[4]),
    ]
    for load in loads:
        load.start()
    shifted = pltpu.roll(jnp.broadcast_to(small_ref[:, : 2 * taps], (taps, 2 * taps)), 0, 1, stride=1, stride_axis=0)
    toeplitz = halves(shifted)
    high_ref[...], low_ref[...] = toeplitz

    code = small_ref[:, 2 * taps : 2 * taps + rows].astype(jnp.int32)
    owner, sub = code // BIN_DEV, code % BIN_DEV
    owners = NY * NU * NW * NC
    named = lax.broadcasted_iota(jnp.int32, (owners, rows), 0) == owner
    named = jnp.where(named, 1.0, 0.0)
    earlier = lax.broadcasted_iota(jnp.int32, (rows, rows), 0) < lax.broadcasted_iota(jnp.int32, (rows, rows), 1)
    earlier = jnp.where(earlier, 1.0, 0.0).astype(jnp.bfloat16)
    rank = jnp.sum(named * dot(named.astype(jnp.bfloat16), earlier), axis=0, keepdims=True).astype(jnp.int32)
    core, w = owner % NC, owner // NC % NW
    u, y = owner // (NC * NW) % NU, owner // (NC * NW * NU)
    peer = (y * NW + w) * NC + core
    within = u * CAP + rank
    slot = peer * SLOTS + within
    slot_ref[...] = slot
    to_peer = lax.broadcasted_iota(jnp.int32, (PEERS, rows), 0) == peer
    to_peer = jnp.where(to_peer, (sub + 1).astype(jnp.float32), 0.0).astype(jnp.bfloat16)
    column = lax.broadcasted_iota(jnp.int32, (LANES, rows), 0)
    shelf = lax.rem(lax.axis_index(NEAR), SHELVES) * SLOTS
    in_column = jnp.where(column == within + shelf, 1.0, 0.0).astype(jnp.bfloat16)
    label_ref[...] = lax.dot_general(
        to_peer, in_column, (((1,), (1,)), ((), ())), preferred_element_type=jnp.float32
    )

    loads[0].wait()
    loads[1].wait()
    stacked = jnp.concatenate([traces_ref[:, b * taps : (b + 1) * taps] for b in range(count)], axis=0)
    spread = dot_split(halves(stacked), toeplitz)
    pieces = [
        spread[b * rows : (b + 1) * rows, :taps] + spread[(b - 1) * rows : b * rows, taps:] for b in range(1, count)
    ]
    edge_ref[:, :taps] = spread[:rows, :taps]
    edge_ref[:, taps : 2 * taps] = pieces[0]
    edge_ref[:, 2 * taps : 3 * taps] = pieces[-1]
    edge_ref[:, 3 * taps :] = spread[(count - 1) * rows :, taps:]
    loads[2].wait()
    quarters = [map_ref[:, c * LANES : (c + 1) * LANES] for c in range(half // LANES)]
    placed = place_slots(slot, move_out(jnp.concatenate(pieces, axis=1), quarters))
    for c, placed_ref in enumerate(placed_refs):
        placed_ref[...] = placed[:, c * LANES : (c + 1) * LANES]
    loads[3].wait()
    loads[4].wait()


def outer_kernel(before_ref, after_ref, high_ref, low_ref, edge_ref, edge_map_ref, slot_ref, label_ref, *rest):
    *placed_refs, out_ref = rest
    taps = before_ref.shape[1]
    parts = taps // LANES
    length = out_ref.shape[0] // PEERS
    slot = slot_ref[...]

    def put(c, placed):
        for peer in range(PEERS):
            start = peer * length + c * SLOTS
            out_ref[start : start + SLOTS, :] = placed[peer * SLOTS : (peer + 1) * SLOTS, :]

    def moved(k, window):
        return move_out(window, [edge_map_ref[:, (k + i) * LANES : (k + i + 1) * LANES] for i in range(parts)])

    early = dot_split(halves(before_ref[...]), (high_ref[:, taps:], low_ref[:, taps:])) + edge_ref[:, :taps]
    late = dot_split(halves(after_ref[...]), (high_ref[:, :taps], low_ref[:, :taps])) + edge_ref[:, 3 * taps :]
    late = jnp.where(lax.axis_index("section") == lax.axis_size("section") - 1, 0.0, late)
    first = moved(0, jnp.concatenate([early, edge_ref[:, taps : 2 * taps]], axis=1))
    last = moved(parts, jnp.concatenate([edge_ref[:, 2 * taps : 3 * taps], late], axis=1))
    placed = place_slots(slot, jnp.concatenate([first, last], axis=1))
    places = [*range(parts), *range(parts + len(placed_refs), 2 * parts + len(placed_refs))]
    for i, c in enumerate(places):
        put(c, placed[:, i * LANES : (i + 1) * LANES])
    for c, placed_ref in enumerate(placed_refs):
        put(parts + c, placed_ref)
    for peer in range(PEERS):
        out_ref[(peer + 1) * length - 1 : (peer + 1) * length, :] = label_ref[peer : peer + 1, :]


def combine_kernel(arrived_ref, out_ref):
    length = arrived_ref.shape[0] // PEERS
    out_length = out_ref.shape[0] // NU
    parts = length // SLOTS
    shelves = []
    for first in range(0, PEERS, SHELVES):
        row = sum(arrived_ref[(peer + 1) * length - 1 : (peer + 1) * length, :] for peer in range(first, first + SHELVES))
        shelves.append(row)
    labels = jnp.concatenate(shelves, axis=1)
    slots = PEERS * SLOTS
    shape = (NU * BIN_DEV, slots)
    row = lax.broadcasted_iota(jnp.int32, shape, 0)
    column = lax.broadcasted_iota(jnp.int32, shape, 1)
    bin_label = (row % BIN_DEV + 1).astype(jnp.float32)
    hit = (labels == bin_label) & (row // BIN_DEV == column % SLOTS // CAP)
    member = jnp.where(hit, 1.0, 0.0).astype(jnp.bfloat16)
    for c in range(0, parts, 2):
        pair = []
        for k in (c, c + 1):
            starts = [peer * length + k * SLOTS for peer in range(PEERS)]
            pair.append(jnp.concatenate([arrived_ref[start : start + SLOTS, :] for start in starts], axis=0))
        total = dot_exact(member, jnp.concatenate(pair, axis=1))
        for k in (0, 1):
            for u in range(NU):
                start = u * out_length + (c + k) * BIN_DEV
                out_ref[start : start + BIN_DEV, :] = total[
                    u * BIN_DEV : (u + 1) * BIN_DEV, k * LANES : (k + 1) * LANES
                ]
    column = lax.broadcasted_iota(jnp.int32, (NU, slots), 1)
    of_owner = (lax.broadcasted_iota(jnp.int32, (NU, slots), 0) == column % SLOTS // CAP) & (labels > 0.0)
    of_owner = jnp.where(of_owner, 1.0, 0.0).astype(jnp.bfloat16)
    of_bin = labels == (lax.broadcasted_iota(jnp.int32, (LANES, slots), 0) + 1).astype(jnp.float32)
    of_bin = jnp.where(of_bin, 1.0, 0.0).astype(jnp.bfloat16)
    fold = lax.dot_general(of_owner, of_bin, (((1,), (1,)), ((), ())), preferred_element_type=jnp.float32)
    for u in range(NU):
        out_ref[(u + 1) * out_length - 1 : (u + 1) * out_length, :] = fold[u : u + 1, :]


def finish_kernel(arrived_ref, out_ref):
    length = arrived_ref.shape[0] // NU
    fold = sum(arrived_ref[(u + 1) * length - 1 : (u + 1) * length, :] for u in range(NU))
    diagonal = lax.broadcasted_iota(jnp.int32, (BIN_DEV, LANES), 0) == lax.broadcasted_iota(jnp.int32, (BIN_DEV, LANES), 1)
    counts = jnp.sum(jnp.where(diagonal, fold, 0.0), axis=1, keepdims=True)
    scale = jnp.broadcast_to(1.0 / jnp.sqrt(jnp.maximum(counts, 1.0)), (BIN_DEV, LANES))
    for c in range(length // BIN_DEV):
        starts = [u * length + c * BIN_DEV for u in range(NU)]
        total = sum(arrived_ref[start : start + BIN_DEV, :] for start in starts)
        out_ref[:, c * LANES : (c + 1) * LANES] = total * scale


VMEM = pl.BlockSpec(memory_space=pltpu.VMEM)
ANY = pl.BlockSpec(memory_space=pl.ANY)
LIMIT = 24 * 1024 * 1024
INNER_LIMIT = 53760


def f32(*shape):
    return jax.ShapeDtypeStruct(shape, jnp.float32)


def correct_inner(small, traces, sample_map):
    rows, width = traces.shape
    taps = (small.shape[1] - LANES) // 2
    inner = (width - 2 * taps) // LANES
    return pl.pallas_call(
        inner_kernel,
        out_shape=(
            jax.ShapeDtypeStruct((taps, 2 * taps), jnp.bfloat16),
            jax.ShapeDtypeStruct((taps, 2 * taps), jnp.bfloat16),
            f32(rows, 4 * taps),
            jax.ShapeDtypeStruct((rows, 2 * taps), jnp.int32),
            jax.ShapeDtypeStruct((1, rows), jnp.int32),
            f32(PEERS, LANES),
        )
        + (f32(PEERS * SLOTS, LANES),) * inner,
        in_specs=[VMEM, ANY, ANY],
        out_specs=(VMEM,) * (6 + inner),
        scratch_shapes=[
            pltpu.VMEM((rows, width), jnp.float32),
            pltpu.VMEM((rows, inner * LANES), jnp.int32),
            pltpu.SemaphoreType.DMA((5,)),
        ],
        name="correct_inner",
        cost_estimate=pl.CostEstimate(flops=500_000_000, bytes_accessed=2_000_000, transcendentals=0),
        compiler_params=pltpu.CompilerParams(vmem_limit_bytes=INNER_LIMIT * 1024),
    )(small, traces, sample_map)


def on_vmem(kernel, shape, name, *operands):
    return pl.pallas_call(
        kernel,
        out_shape=f32(*shape),
        in_specs=[VMEM] * len(operands),
        out_specs=VMEM,
        name=name,
        compiler_params=pltpu.CompilerParams(vmem_limit_bytes=LIMIT),
    )(*operands)


def passed_along(value, axis, steps):
    count = lax.axis_size(axis)
    leading, last = (max(0, -steps), min(count, count - steps))
    return lax.ppermute(value, axis, [(source, source + steps) for source in range(leading, last)])


def exchanged(rows, axes):
    count, lanes = rows.shape
    sent = rows.reshape(count, 1, lanes)
    return lax.all_to_all(sent, axes, split_axis=0, concat_axis=0, tiled=True).reshape(count, lanes)


def per_device(traces, filters, owners, sub_bins, sample_map):
    rows, width = traces.shape
    taps = filters.shape[1]
    before = passed_along(traces[:, width - taps :], "section", 1)
    after = passed_along(traces[:, :taps], "section", -1)
    around = ((0, 0), (2 * taps, LANES - rows))
    owner, sub = jnp.pad(owners.reshape(1, rows), around), jnp.pad(sub_bins.reshape(1, rows), around)
    small = jnp.pad(filters, ((0, 0), (0, taps + LANES))) + (owner * BIN_DEV + sub).astype(jnp.float32)
    kept = correct_inner(small, traces, sample_map)
    parts = width // LANES
    sent = on_vmem(outer_kernel, (PEERS * (parts * SLOTS + 1), LANES), "correct_outer", before, after, *kept)
    near = exchanged(sent, NEAR)
    summed = on_vmem(combine_kernel, (NU * (parts * BIN_DEV + 1), LANES), "combine", near)
    arrived = exchanged(summed, "u")
    return on_vmem(finish_kernel, (BIN_DEV, width), "finish", arrived)


def solution(mesh):
    fine = Mesh(mesh.devices.reshape(mesh.devices.shape[0], NY, NU, NW, NC), ("section",) + BINS)
    in_specs = (
        P(BINS, "section"),
        P(BINS, None),
        P(BINS, None),
        P(BINS),
        P(BINS, "section"),
    )
    return jax.shard_map(
        per_device, mesh=fine, in_specs=in_specs, out_specs=P(BINS, "section"), check_vma=False
    )
```
